32 devices in a mesh: rep: 2 (over y), dev: 16 (over z, x, core).
Axes of the slice: x: 2, y: 2, z: 4, core: 2. Of those that a mesh axis runs over, the one named last changes fastest.
Arguments:
- tokens: bfloat16 [4096, 3584], P(('rep', 'dev')), parts along dimension 0, may hold values from -6 to 6
- norm_gain: float32 [3584], replicated, may hold values from 0.5 to 1.5
- kv_weight: bfloat16 [3584, 576], P('dev'), may hold values from -0.09375 to 0.09375
- key_value_gain: float32 [512], replicated, may hold values from 0.5 to 1.5
- gate_weight: bfloat16 [3584, 4096], P(None, 'dev'), may hold values from -0.09375 to 0.09375
- up_weight: bfloat16 [3584, 4096], P(None, 'dev'), may hold values from -0.09375 to 0.09375
- down_weight: bfloat16 [16384, 896], P('dev'), may hold values from -0.1875 to 0.1875
- expert_index: int32 [4096, 2], P(('rep', 'dev')), parts along dimension 0, may hold values from 0 to 3, all different within a row; in each aligned block of 128 rows (0 to 127, 128 to 255, ...) at most 128 rows name the same one
- route_gate: float32 [4096, 2], P(('rep', 'dev')), parts along dimension 0, may hold values from 0.2 to 1
- owner: int32 [4096, 1], P(('rep', 'dev')), parts along dimension 0, may hold values from 0 to 15; in each aligned block of 128 rows (0 to 127, 128 to 255, ...) at most 16 rows name the same one
Outputs:
- moe_out: bfloat16 [4096, 3584], P(('rep', 'dev')), parts along dimension 0
- latent_cache: bfloat16 [8192, 576], P(('rep', 'dev')), parts along dimension 0
The draws below stay inside these ranges and needn't reach their ends.
There are 2 independent parts, one for each index of `rep`. The reference program is written for one: setup_inputs(seed, part) draws one part's arguments, and reference() takes and returns one part's arrays. A program takes and returns all parts, laid end to end along the dimension named above; an argument that names none is the same for every part. Nothing has to cross between parts.
Inputs may be any that keep to these rules, and one draw needn't show every extreme that they name: `expert_index`: the 2 experts of a token differ. Among the entries of the 128 tokens of one device, no expert is named more than 128 times, and some expert of some device is named exactly 128 times. At most 16 tokens of one device name the same owner, and in some device exactly 16 do.
All inputs are finite; a program needn't handle non-finite values.
Results may differ from the reference program's by a relative error of at most 0.0071.
Values may be sent and summed in bfloat16 or wider, within the bound.
No kernel may reach another device: no remote copies, remote signals or barrier semaphores. Data moves between devices by JAX's collectives and lax.ppermute only.
A program may use at most 128 MiB of HBM per device.

```python
import math
import jax
import jax.numpy as jnp
import numpy as np
from jax import lax

D = 3584
FF = 1024
KEY_VALUE_RANK = 512
ROUTES = 2
TOK_DEV = 128
GROUP = 4
EXPERTS = 4
CAP = 128
PUSH_CAP = 16
LAT = 576
TOKENS = 2048


def levels(key, extent, cuts, smallest, top_value):
    gain, own = 1.0, jax.random.fold_in(key, 6)
    for position, blocks in cuts:
        steps = jnp.exp(jax.random.uniform(jax.random.fold_in(own, position), (blocks,), jnp.float32, smallest / len(cuts), top_value / len(cuts)))
        gain = gain * jnp.repeat(steps, extent[position] // blocks).reshape([-1 if axis == position else 1 for axis in range(len(extent))])
    return gain


def shared_out(rng, own, number, rows, count, top, limit, skew):
    ranking = jax.random.permutation(rng, count)
    packed, usual = load_shares(count, rows * top, limit, skew, True), load_shares(count, rows * top, limit, skew, False)
    places = jnp.arange(count)

    def named(sizes, rotation):
        used = int((sizes > 0).sum())
        fixed = max(1, used // 4)
        shifted = fixed + (places - fixed + rotation * (used - fixed)) % max(1, count - fixed)
        return jnp.zeros((count,), jnp.int32).at[ranking[jnp.where(places < fixed, places, shifted)]].set(jnp.asarray(sizes, jnp.int32))

    sizes = jnp.where(number % 4 == 0, named(packed, number // 4), named(usual, number - number // 4 - 1))
    mixed = jax.random.permutation(jax.random.fold_in(own, 3), count)
    source_of, taker = mixed[0:count // 2 * 2:2], mixed[1:count // 2 * 2:2]
    margin = jnp.minimum(sizes[source_of] - 1, limit - sizes[taker]) // 2
    margin = jnp.where((source_of == ranking[0]) | (taker == ranking[0]) | (sizes[taker] == 0), 0, jnp.maximum(margin, 0))
    shifted = jax.random.randint(jax.random.fold_in(own, 4), (count // 2,), 0, 1 << 20) % (margin + 1)
    sizes = sizes.at[source_of].add(-shifted).at[taker].add(shifted)
    items = jnp.searchsorted(jnp.cumsum(sizes), jnp.arange(rows * top), side="right").astype(jnp.int32)
    table = items.reshape(top, rows).T
    table = table[jax.random.permutation(jax.random.fold_in(own, 1), rows)]
    rotation = jax.random.randint(jax.random.fold_in(own, 2), (rows, 1), 0, top)
    return jnp.take_along_axis(table, (jnp.arange(top)[None, :] + rotation) % top, axis=1)


def load_shares(count, total, bound, slope, full):
    weights = [(1 << 20) // math.isqrt(grade ** slope) + 1 for grade in range(1, count + 1)]
    largest = bound if full else min(bound, max(-(-total // count), total * weights[0] // sum(weights)))
    least = 1 if total - largest >= count - 1 else 0
    counts, surplus = [largest] + [least] * (count - 1), total - largest - least * (count - 1)
    while surplus > 0:
        movable = [i for i in range(1, count) if counts[i] < largest] or [i for i in range(1, count) if counts[i] < bound]
        whole, remaining = sum([weights[i] for i in movable]), surplus
        for i in movable:
            more = min(bound - counts[i], max(1, remaining * weights[i] // whole), surplus)
            counts[i] = counts[i] + more
            surplus = surplus - more
    return np.array(counts)


def noise(rng, dims, spread, most, shards=(), kind=jnp.bfloat16):
    drawn = jax.random.normal(rng, dims, jnp.float32) * spread
    if len(shards) > 0:
        drawn = levels(rng, dims, shards, -0.22, 0.18) * drawn
    return jnp.clip(drawn, min=-most, max=most).astype(kind)


def setup_inputs(seed: int = 0, part: int = 0) -> dict:
    streams_of = jax.random.split(jax.random.key(seed), 11)
    part_splits = jax.random.split(jax.random.fold_in(streams_of[10], part), 11)
    tokens = noise(part_splits[0], (TOKENS, D), 1.0, 6.0, ((0, 16),))
    norm_gain = jnp.clip(1.0 + 0.1 * jax.random.normal(streams_of[1], (D,), jnp.float32), 0.5, 1.5)
    kv_weight = noise(streams_of[2], (D, LAT), D ** -0.5, 0.09375, ((0, 16),))
    key_value_gain = jnp.clip(1.0 + 0.1 * jax.random.normal(streams_of[3], (KEY_VALUE_RANK,), jnp.float32), 0.5, 1.5)
    gate_weight = noise(streams_of[4], (D, EXPERTS * FF), D ** -0.5, 0.09375, ((1, 16),))
    up_weight = noise(streams_of[5], (D, EXPERTS * FF), D ** -0.5, 0.09375, ((1, 16),))
    down_weight = noise(streams_of[6], (EXPERTS * GROUP * FF, D // GROUP), FF ** -0.5, 0.1875, ((0, 16),))
    expert_index_keys = jax.random.split(jax.random.fold_in(part_splits[7], 1), TOKENS // TOK_DEV)
    expert_index_turns = jax.random.permutation(jax.random.fold_in(part_splits[7], 3), TOKENS // TOK_DEV)
    expert_index = jax.vmap(lambda own, number: shared_out(jax.random.fold_in(part_splits[7], 2), own, number, TOK_DEV, EXPERTS, ROUTES, CAP, 2))(expert_index_keys, expert_index_turns).reshape((TOKENS, ROUTES))
    route_gate = jnp.clip(jnp.exp(math.log(1.0) - 1.609438 * jax.random.uniform(part_splits[8], (TOKENS, ROUTES), jnp.float32) ** levels(part_splits[8], (TOKENS, ROUTES), ((0, 16),), -0.2, 0.2)), 0.2, 1.0)
    owner_keys = jax.random.split(jax.random.fold_in(part_splits[9], 1), TOKENS // TOK_DEV)
    owner_turns = jax.random.permutation(jax.random.fold_in(part_splits[9], 3), TOKENS // TOK_DEV)
    owner = jax.vmap(lambda own, number: shared_out(jax.random.fold_in(part_splits[9], 2), own, number, TOK_DEV, EXPERTS * GROUP, 1, PUSH_CAP, 2))(owner_keys, owner_turns).reshape((TOKENS, 1))
    return dict(tokens=tokens, norm_gain=norm_gain, kv_weight=kv_weight, key_value_gain=key_value_gain, gate_weight=gate_weight, up_weight=up_weight, down_weight=down_weight, expert_index=expert_index, route_gate=route_gate, owner=owner)


eps = 1e-06
rope_theta = 50000.0

def root_mean_scale(values, gain_vector):
    mean_sq = lax.optimization_barrier(jnp.mean(values * values, axis=-1, keepdims=True))
    return values * lax.rsqrt(mean_sq + eps) * gain_vector

def apply_rotary_keys(key_part, token_positions):
    half_width = key_part.shape[-1] // 2
    frequency = rope_theta ** (-jnp.arange(half_width, dtype=jnp.float32) * 2.0 / key_part.shape[-1])
    angles = token_positions.astype(jnp.float32)[:, None] * frequency[None, :]
    cos_part = jnp.cos(angles)
    sin_part = jnp.sin(angles)
    front_half = key_part[:, :half_width]
    back_half = key_part[:, half_width:]
    return jnp.concatenate([front_half * cos_part - back_half * sin_part, back_half * cos_part + front_half * sin_part], axis=-1)

def block_ranks(labels, label_count):
    onehot = (labels[..., None] == jnp.arange(label_count, dtype=jnp.int32)).astype(jnp.int32)
    before = jnp.cumsum(onehot, axis=1, dtype=jnp.int32) - onehot
    return lax.optimization_barrier(jnp.sum(before * onehot, axis=-1, dtype=jnp.int32))

def reference(tokens, norm_gain, kv_weight, key_value_gain, gate_weight, up_weight, down_weight, expert_index, route_gate, owner):
    device_count = EXPERTS * GROUP
    normed = root_mean_scale(tokens.astype(jnp.float32), norm_gain).astype(jnp.bfloat16)
    unnormed_latent = jnp.dot(normed, kv_weight, preferred_element_type=jnp.float32)
    token_positions = jnp.arange(TOKENS, dtype=jnp.int32) % TOK_DEV
    latent_vector = jnp.concatenate([root_mean_scale(unnormed_latent[:, :KEY_VALUE_RANK], key_value_gain), apply_rotary_keys(unnormed_latent[:, KEY_VALUE_RANK:], token_positions)], axis=-1).astype(jnp.bfloat16)
    owners = owner.reshape(device_count, TOK_DEV)
    owner_rank = block_ranks(owners, device_count)
    source = jnp.arange(device_count * TOK_DEV, dtype=jnp.int32).reshape(device_count, TOK_DEV) // TOK_DEV
    cache_rows = jnp.zeros((device_count, device_count, PUSH_CAP, LAT), jnp.bfloat16)
    cache_rows = cache_rows.at[owners, source, owner_rank].set(latent_vector.reshape(device_count, TOK_DEV, LAT))
    latent_cache = cache_rows.reshape(device_count * device_count * PUSH_CAP, LAT)
    entries = TOK_DEV * ROUTES
    experts = expert_index.reshape(device_count, entries)
    slot_index = block_ranks(experts, EXPERTS)
    entry_source = jnp.arange(device_count * entries, dtype=jnp.int32).reshape(device_count, entries) // entries
    flat_pos = entry_source * CAP + slot_index
    token_ids = (jnp.arange(device_count * entries, dtype=jnp.int32) // ROUTES).reshape(device_count, entries)
    row_table = jnp.full((EXPERTS, device_count * CAP), TOKENS, jnp.int32).at[experts, flat_pos].set(token_ids)
    weights_tab = jnp.zeros((EXPERTS, device_count * CAP), jnp.float32).at[experts, flat_pos].set(route_gate.reshape(device_count, entries))
    padded = jnp.concatenate([normed, jnp.zeros((1, D), jnp.bfloat16)], axis=0)
    gate_all = gate_weight.reshape(D, EXPERTS, FF)
    up_all = up_weight.reshape(D, EXPERTS, FF)
    down_all = down_weight.reshape(EXPERTS, GROUP, FF, D // GROUP)

    def one_expert(running, expert_id):
        expert_rows = padded[row_table[expert_id]]
        gate_part = jnp.dot(expert_rows, lax.dynamic_index_in_dim(gate_all, expert_id, 1, False), preferred_element_type=jnp.float32)
        up_part = jnp.dot(expert_rows, lax.dynamic_index_in_dim(up_all, expert_id, 1, False), preferred_element_type=jnp.float32)
        hidden = (jax.nn.silu(gate_part) * up_part).astype(jnp.bfloat16)
        down_matrix = jnp.transpose(lax.dynamic_index_in_dim(down_all, expert_id, 0, False), (1, 0, 2)).reshape(FF, D)
        outputs = jnp.dot(hidden, down_matrix, preferred_element_type=jnp.float32).astype(jnp.bfloat16)
        running = running.at[row_table[expert_id]].add(weights_tab[expert_id][:, None] * outputs.astype(jnp.float32))
        return (running, None)
    running = jnp.zeros((TOKENS + 1, D), jnp.float32)
    running, unused = lax.scan(one_expert, running, jnp.arange(EXPERTS, dtype=jnp.int32))
    moe_out = running[:TOKENS].astype(jnp.bfloat16)
    return (moe_out, latent_cache)
```

```python
import functools

import jax
import jax.numpy as jnp
from jax import lax
from jax.experimental import pallas as pl
from jax.experimental.pallas import tpu as pltpu
from jax.sharding import PartitionSpec as P

KEY_VALUE_RANK = 512
ROUTES = 2
LOG_GROUP = 2
GROUP = 4
LINE = 4


eps = 1e-06
rope_theta = 50000.0


def swapped(value, axis, stride):
    return lax.ppermute(value, axis, [(i, i ^ 1 << stride) for i in range(lax.axis_size(axis))])


def root_mean_scale(values, gain_vector):
    mean_sq = jnp.mean(values * values, axis=-1, keepdims=True)
    return values * lax.rsqrt(mean_sq + eps) * gain_vector


def apply_rotary_keys(key_part, token_positions):
    half_width = key_part.shape[-1] // 2
    frequency = rope_theta ** (
        -jnp.arange(half_width, dtype=jnp.float32) * 2.0 / key_part.shape[-1]
    )
    angles = token_positions.astype(jnp.float32)[:, None] * frequency[None, :]
    cos_part = jnp.cos(angles)
    sin_part = jnp.sin(angles)
    front_half = key_part[:, :half_width]
    back_half = key_part[:, half_width:]
    return jnp.concatenate(
        [
            front_half * cos_part - back_half * sin_part,
            back_half * cos_part + front_half * sin_part,
        ],
        axis=-1,
    )


def block_ranks(labels, label_count):
    onehot = (labels[..., None] == jnp.arange(label_count, dtype=jnp.int32)).astype(jnp.int32)
    before = jnp.cumsum(onehot, axis=1, dtype=jnp.int32) - onehot
    return jnp.sum(before * onehot, axis=-1, dtype=jnp.int32)


def latent_rows(raw_latent, key_value_gain):
    token_positions = jnp.arange(raw_latent.shape[0], dtype=jnp.int32)
    return jnp.concatenate(
        [
            root_mean_scale(raw_latent[:, :KEY_VALUE_RANK], key_value_gain),
            apply_rotary_keys(raw_latent[:, KEY_VALUE_RANK:], token_positions),
        ],
        axis=-1,
    ).astype(jnp.bfloat16)


def cache_send_rows(latent_vector, owner, device_count, push_cap):
    target = owner[:, 0]
    rank_index = block_ranks(target[None, :], device_count)[0]
    return (
        jnp.zeros((device_count * push_cap, latent_vector.shape[1]), jnp.bfloat16)
        .at[target * push_cap + rank_index]
        .set(latent_vector)
    )


def packed_shards(
    tokens,
    norm_gain,
    kv_weight,
    key_value_gain,
    gate_weight,
    up_weight,
    down_weight,
    expert_index,
    route_gate,
    owner,
):
    device_count = lax.axis_size("dev")
    experts_count = device_count // GROUP
    tok_rows = tokens.shape[0]
    features = tokens.shape[1]
    capacity = 2 * tok_rows * ROUTES // experts_count
    push_cap = max(2, 2 * tok_rows // device_count)
    own_index = lax.axis_index("dev")
    normed = root_mean_scale(tokens.astype(jnp.float32), norm_gain).astype(jnp.bfloat16)
    flat_experts = expert_index.reshape(1, tok_rows * ROUTES)
    slot_index = block_ranks(flat_experts, experts_count)[0]
    expert_of = flat_experts[0]
    token_of = jnp.arange(tok_rows * ROUTES, dtype=jnp.int32) // ROUTES
    position = expert_of * capacity + slot_index
    packed = (
        jnp.zeros((experts_count * capacity, features), jnp.bfloat16)
        .at[position]
        .set(normed[token_of])
    )
    copies = jnp.broadcast_to(
        packed.reshape(experts_count, 1, capacity, features),
        (experts_count, GROUP, capacity, features),
    )
    received = lax.all_to_all(
        copies.reshape(device_count * capacity, features),
        "dev",
        split_axis=0,
        concat_axis=0,
        tiled=True,
    )
    gate_part = jnp.dot(received, gate_weight, preferred_element_type=jnp.float32)
    up_part = jnp.dot(received, up_weight, preferred_element_type=jnp.float32)
    hidden = (jax.nn.silu(gate_part) * up_part).astype(jnp.bfloat16)
    for bit_number in range(LOG_GROUP):
        partner = swapped(hidden, "dev", bit_number)
        upper_half = own_index >> bit_number & 1 == 1
        hidden = jnp.where(
            upper_half,
            jnp.concatenate([partner, hidden], axis=1),
            jnp.concatenate([hidden, partner], axis=1),
        )
    outputs = jnp.dot(hidden, down_weight, preferred_element_type=jnp.float32).astype(jnp.bfloat16)
    returned = lax.all_to_all(
        outputs.reshape(device_count, capacity, outputs.shape[1]),
        "dev",
        split_axis=0,
        concat_axis=2,
        tiled=True,
    )
    result = returned.reshape(capacity, experts_count, features)
    picked = result[slot_index, expert_of]
    weighted = route_gate.reshape(tok_rows * ROUTES, 1) * picked.astype(jnp.float32)
    combined = jnp.sum(weighted.reshape(tok_rows, ROUTES, features), axis=1)
    moe_out = combined.astype(jnp.bfloat16)
    raw_latent = jnp.dot(
        normed,
        lax.all_gather(kv_weight, "dev", axis=0, tiled=True),
        preferred_element_type=jnp.float32,
    )
    send_rows = cache_send_rows(
        latent_rows(raw_latent, key_value_gain), owner, device_count, push_cap
    )
    latent_cache = lax.all_to_all(send_rows, "dev", split_axis=0, concat_axis=0, tiled=True)
    return (moe_out, latent_cache)


def hidden_kernel(
    place_ref,
    own_ref, a_ref, b_ref, c_ref, d_ref, e_ref,
    g0_ref, g1_ref, g2m_ref, g2o_ref, g3m_ref, g3o_ref,
    u0_ref, u1_ref, u2m_ref, u2o_ref, u3m_ref, u3o_ref,
    hidden_ref,
    rows_buf, gate_buf, up_buf, row_sems, gate_sems, up_sems,
):
    place, rep, is_end = place_ref[0], place_ref[1], place_ref[2]
    half = rows_buf.shape[2] // 2
    own_copy = pltpu.make_async_copy(own_ref, rows_buf.at[0], row_sems.at[0])
    a_copy = pltpu.make_async_copy(a_ref, rows_buf.at[1], row_sems.at[1])
    own_copy.start()
    a_copy.start()

    @pl.when(is_end == 1)
    def _():
        pltpu.make_async_copy(c_ref, rows_buf.at[2], row_sems.at[2]).start()
        pltpu.make_async_copy(e_ref, rows_buf.at[3], row_sems.at[3]).start()

    @pl.when(is_end == 0)
    def _():
        pltpu.make_async_copy(d_ref, rows_buf.at[2], row_sems.at[2]).start()
        pltpu.make_async_copy(b_ref, rows_buf.at[3], row_sems.at[3]).start()

    def fetch(refs, buf, sems):
        whole0, whole1, mine2, other2, mine3, other3 = refs
        at_mine, at_other = pl.ds(rep * half, half), pl.ds((1 - rep) * half, half)
        copies = [
            [pltpu.make_async_copy(whole0, buf.at[place], sems.at[0])],
            [pltpu.make_async_copy(whole1, buf.at[place ^ 1], sems.at[1])],
            [
                pltpu.make_async_copy(mine2, buf.at[place ^ 2, at_mine], sems.at[2]),
                pltpu.make_async_copy(other2, buf.at[place ^ 2, at_other], sems.at[3]),
            ],
            [
                pltpu.make_async_copy(mine3, buf.at[place ^ 3, at_mine], sems.at[4]),
                pltpu.make_async_copy(other3, buf.at[place ^ 3, at_other], sems.at[5]),
            ],
        ]
        return copies

    gates = fetch((g0_ref, g1_ref, g2m_ref, g2o_ref, g3m_ref, g3o_ref), gate_buf, gate_sems)
    ups = fetch((u0_ref, u1_ref, u2m_ref, u2o_ref, u3m_ref, u3o_ref), up_buf, up_sems)
    for k in range(GROUP):
        for copy in gates[k] + ups[k]:
            copy.start()
    own_copy.wait()
    a_copy.wait()

    @pl.when(is_end == 1)
    def _():
        pltpu.make_async_copy(c_ref, rows_buf.at[2], row_sems.at[2]).wait()
        pltpu.make_async_copy(e_ref, rows_buf.at[3], row_sems.at[3]).wait()

    @pl.when(is_end == 0)
    def _():
        pltpu.make_async_copy(d_ref, rows_buf.at[2], row_sems.at[2]).wait()
        pltpu.make_async_copy(b_ref, rows_buf.at[3], row_sems.at[3]).wait()

    units = gate_buf.shape[2]
    tok_rows, features = rows_buf.shape[1:]
    for k in range(GROUP):
        for copy in gates[k] + ups[k]:
            copy.wait()
        slot = place ^ k
        at_units = pl.ds(pl.multiple_of(slot * units, units), units)

        @pl.loop(0, LINE // 2)
        def _(pair):
            rows = rows_buf[pl.ds(2 * pair, 2)].reshape(2 * tok_rows, features)
            gate_part = jnp.dot(rows, gate_buf[slot], preferred_element_type=jnp.float32)
            up_part = jnp.dot(rows, up_buf[slot], preferred_element_type=jnp.float32)
            part = (gate_part / (1.0 + jnp.exp(-gate_part)) * up_part).astype(jnp.bfloat16)
            hidden_ref[pl.ds(2 * pair, 2), :, at_units] = part.reshape(2, tok_rows, units)


def hidden_units(place, rows, gates, ups):
    tok_rows, features = rows[0].shape
    units = gates[0].shape[1]
    any_space = pl.BlockSpec(memory_space=pl.ANY)
    weight_bytes = 2 * GROUP * features * units * 2
    return pl.pallas_call(
        hidden_kernel,
        out_shape=jax.ShapeDtypeStruct((LINE, tok_rows, GROUP * units), jnp.bfloat16),
        in_specs=[pl.BlockSpec(memory_space=pltpu.SMEM)] + [any_space] * 18,
        out_specs=pl.BlockSpec(memory_space=pltpu.VMEM),
        scratch_shapes=[
            pltpu.VMEM((LINE, tok_rows, features), jnp.bfloat16),
            pltpu.VMEM((GROUP, features, units), jnp.bfloat16),
            pltpu.VMEM((GROUP, features, units), jnp.bfloat16),
            pltpu.SemaphoreType.DMA((LINE,)),
            pltpu.SemaphoreType.DMA((6,)),
            pltpu.SemaphoreType.DMA((6,)),
        ],
        compiler_params=pltpu.CompilerParams(vmem_limit_bytes=48 * 1024 * 1024),
        cost_estimate=pl.CostEstimate(
            flops=4 * LINE * tok_rows * features * GROUP * units,
            bytes_accessed=weight_bytes + LINE * tok_rows * features * 2,
            transcendentals=LINE * tok_rows * GROUP * units,
        ),
        name="hidden_units",
    )(place, *rows, *gates, *ups)


def down_kernel(parts, place_ref, hidden_ref, scale_ref, *refs):
    down_refs = refs[:parts]
    out_refs = refs[parts : parts + LINE]
    down_buf, sems = refs[parts + LINE :]
    core, rep = place_ref[0] & 1, place_ref[1]
    if parts == 2:
        copies = [
            pltpu.make_async_copy(down_refs[0], down_buf.at[core], sems.at[0]),
            pltpu.make_async_copy(down_refs[1], down_buf.at[1 - core], sems.at[1]),
        ]
    else:
        half = down_buf.shape[1] // 2
        at_mine, at_other = pl.ds(rep * half, half), pl.ds((1 - rep) * half, half)
        copies = [
            pltpu.make_async_copy(down_refs[0], down_buf.at[core, at_mine], sems.at[0]),
            pltpu.make_async_copy(down_refs[1], down_buf.at[core, at_other], sems.at[1]),
            pltpu.make_async_copy(down_refs[2], down_buf.at[1 - core, at_mine], sems.at[2]),
            pltpu.make_async_copy(down_refs[3], down_buf.at[1 - core, at_other], sems.at[3]),
        ]
    for copy in copies:
        copy.start()
    for copy in copies:
        copy.wait()
    columns = down_buf.shape[2]
    for k in reversed(range(LINE)):
        for column_block in range(2):
            out = jnp.dot(hidden_ref[k], down_buf[column_block], preferred_element_type=jnp.float32)
            out = out.astype(jnp.bfloat16).astype(jnp.float32) * scale_ref[k]
            out_refs[k][:, column_block * columns : (column_block + 1) * columns] = out.astype(
                jnp.bfloat16
            )


def down_products(place, hidden, scale, downs):
    tok_rows, depth = hidden.shape[1:]
    columns = downs[0].shape[1]
    any_space = pl.BlockSpec(memory_space=pl.ANY)
    vmem = pl.BlockSpec(memory_space=pltpu.VMEM)
    return pl.pallas_call(
        functools.partial(down_kernel, len(downs)),
        out_shape=[jax.ShapeDtypeStruct((tok_rows, 2 * columns), jnp.bfloat16)] * LINE,
        in_specs=[pl.BlockSpec(memory_space=pltpu.SMEM), vmem, vmem] + [any_space] * len(downs),
        out_specs=[vmem] * LINE,
        scratch_shapes=[
            pltpu.VMEM((2, depth, columns), jnp.bfloat16),
            pltpu.SemaphoreType.DMA((len(downs),)),
        ],
        compiler_params=pltpu.CompilerParams(vmem_limit_bytes=40 * 1024 * 1024),
        cost_estimate=pl.CostEstimate(
            flops=4 * LINE * tok_rows * depth * columns,
            bytes_accessed=4 * depth * columns + 4 * LINE * tok_rows * columns,
            transcendentals=0,
        ),
        name="down_products",
    )(place, hidden, scale, *downs)


def dense_shards(
    tokens,
    norm_gain,
    kv_weight,
    key_value_gain,
    gate_weight,
    up_weight,
    down_weight,
    expert_index,
    route_gate,
    owner,
):
    device_count = lax.axis_size("dev")
    tok_rows, features = tokens.shape
    push_cap = max(2, 2 * tok_rows // device_count)
    own_index = lax.axis_index("dev")
    rep = lax.axis_index("rep")
    plane, place = own_index // GROUP, own_index % GROUP
    is_end = (plane == 0) | (plane == LINE - 1)
    place_info = jnp.stack([place, rep, is_end.astype(jnp.int32)]).astype(jnp.int32)

    def along(value, pairs):
        return lax.ppermute(value, "dev", pairs)

    def across_line(value, k):
        return along(value, [(i, i ^ GROUP * k) for i in range(device_count)])

    def outer(value):
        return across_line(value, 1)

    def inner(value):
        middle = [(i, i ^ GROUP * 3) for i in range(GROUP, 3 * GROUP)]
        ends = [(i, i) for i in range(device_count) if not GROUP <= i < 3 * GROUP]
        return along(value, middle + ends)

    def other_core(value):
        return along(value, [(i, i ^ 1) for i in range(device_count)])

    def other_chip(value):
        return along(value, [(i, i ^ 2) for i in range(device_count)])

    def other_rep(value):
        return lax.ppermute(value, "rep", [(0, 1), (1, 0)])

    def whole_expert(weight):
        half = weight.shape[0] // 2
        mine = other_chip(lax.dynamic_slice_in_dim(weight, rep * half, half, 0))
        other = other_rep(mine)
        return weight, other_core(weight), mine, other, other_core(mine), other_core(other)

    normed = root_mean_scale(tokens.astype(jnp.float32), norm_gain).astype(jnp.bfloat16)
    a = outer(normed)
    b = inner(normed)
    gates = whole_expert(gate_weight)
    ups = whole_expert(up_weight)
    downs = whole_expert(down_weight)
    c = outer(b)
    d = inner(a)
    e = outer(d)

    expert_weight = jnp.sum(
        jnp.where(
            expert_index[:, :, None] == jnp.arange(LINE, dtype=jnp.int32), route_gate[:, :, None], 0.0
        ),
        axis=1,
    )

    def weight_in(expert):
        return lax.dynamic_slice_in_dim(expert_weight, expert, 1, 1)

    scale = jnp.stack(
        [weight_in(plane)] + [across_line(weight_in(plane ^ k), k) for k in range(1, LINE)]
    )

    kv_pair = other_core(kv_weight)
    kv_pair = jnp.where(
        place & 1 == 1,
        jnp.concatenate([kv_pair, kv_weight]),
        jnp.concatenate([kv_weight, kv_pair]),
    )
    kv_far = other_chip(kv_pair)
    kv_plane = jnp.where(
        place & 2 == 2, jnp.concatenate([kv_far, kv_pair]), jnp.concatenate([kv_pair, kv_far])
    )
    depth = kv_plane.shape[0]

    def plane_features(rows):
        return lax.dynamic_slice_in_dim(rows, plane * depth, depth, 1)

    def latent_part(rows):
        return jnp.dot(rows, kv_plane, preferred_element_type=jnp.float32)

    line_rows = [
        plane_features(normed),
        plane_features(a),
        jnp.where(is_end, plane_features(c), plane_features(d)),
        jnp.where(is_end, plane_features(e), plane_features(b)),
    ]
    latent_parts = latent_part(jnp.concatenate(line_rows)).reshape(LINE, tok_rows, -1)
    raw_latent = latent_parts[0] + sum(
        across_line(latent_parts[k].astype(jnp.bfloat16), k).astype(jnp.float32)
        for k in range(1, LINE)
    )

    hidden = hidden_units(place_info, (normed, a, b, c, d, e), gates, ups)

    def returned(downs):
        parts = down_products(place_info, hidden, scale, downs)
        wide = [part.astype(jnp.float32) for part in parts]

        def narrow(value):
            return value.astype(jnp.bfloat16)

        from_end = outer(parts[3])
        back_d = inner(narrow(wide[2] + from_end.astype(jnp.float32)))
        back_c = outer(parts[2])
        back_b = inner(narrow(wide[3] + back_c.astype(jnp.float32)))
        back_a = outer(narrow(wide[1] + jnp.where(is_end, 0.0, back_d.astype(jnp.float32))))
        return narrow(
            wide[0] + back_a.astype(jnp.float32) + jnp.where(is_end, 0.0, back_b.astype(jnp.float32))
        )

    near = returned(downs[:2])
    far = returned(downs[2:])
    moe_out = jnp.where(
        place & 2 == 2,
        jnp.concatenate([far, near], axis=1),
        jnp.concatenate([near, far], axis=1),
    )
    send_rows = cache_send_rows(
        latent_rows(raw_latent, key_value_gain), owner, device_count, push_cap
    )
    latent_cache = lax.all_to_all(send_rows, "dev", split_axis=0, concat_axis=0, tiled=True)
    return (moe_out, latent_cache)


def solution(mesh):
    in_specs = (
        P(("rep", "dev"), None),
        P(),
        P("dev", None),
        P(),
        P(None, "dev"),
        P(None, "dev"),
        P("dev", None),
        P(("rep", "dev"), None),
        P(("rep", "dev"), None),
        P(("rep", "dev"), None),
    )
    out_specs = (P(("rep", "dev"), None), P(("rep", "dev"), None))
    dense = mesh.shape["dev"] == LINE * GROUP and mesh.shape["rep"] == 2
    shards = dense_shards if dense else packed_shards
    return jax.shard_map(shards, mesh=mesh, in_specs=in_specs, out_specs=out_specs, check_vma=False)
```

```python
import functools

import jax
import jax.numpy as jnp
from jax import lax
from jax.experimental import pallas as pl
from jax.experimental.pallas import tpu as pltpu
from jax.sharding import PartitionSpec as P

KEY_VALUE_RANK = 512
ROUTES = 2
LOG_GROUP = 2
GROUP = 4
LINE = 4
SCALE_COLUMNS = 128
VMEM_GRANT = 56 * 1024 * 1024
BRIEF = pl.CostEstimate(flops=1 << 20, bytes_accessed=1 << 20, transcendentals=0)


eps = 1e-06
rope_theta = 50000.0


def swapped(value, axis, stride):
    return lax.ppermute(value, axis, [(i, i ^ 1 << stride) for i in range(lax.axis_size(axis))])


def root_mean_scale(values, gain_vector):
    mean_sq = jnp.mean(values * values, axis=-1, keepdims=True)
    return values * lax.rsqrt(mean_sq + eps) * gain_vector


def apply_rotary_keys(key_part, token_positions):
    half_width = key_part.shape[-1] // 2
    frequency = rope_theta ** (
        -jnp.arange(half_width, dtype=jnp.float32) * 2.0 / key_part.shape[-1]
    )
    angles = token_positions.astype(jnp.float32)[:, None] * frequency[None, :]
    cos_part = jnp.cos(angles)
    sin_part = jnp.sin(angles)
    front_half = key_part[:, :half_width]
    back_half = key_part[:, half_width:]
    return jnp.concatenate(
        [
            front_half * cos_part - back_half * sin_part,
            back_half * cos_part + front_half * sin_part,
        ],
        axis=-1,
    )


def block_ranks(labels, label_count):
    onehot = (labels[..., None] == jnp.arange(label_count, dtype=jnp.int32)).astype(jnp.int32)
    before = jnp.cumsum(onehot, axis=1, dtype=jnp.int32) - onehot
    return jnp.sum(before * onehot, axis=-1, dtype=jnp.int32)


def latent_rows(raw_latent, key_value_gain):
    token_positions = jnp.arange(raw_latent.shape[0], dtype=jnp.int32)
    return jnp.concatenate(
        [
            root_mean_scale(raw_latent[:, :KEY_VALUE_RANK], key_value_gain),
            apply_rotary_keys(raw_latent[:, KEY_VALUE_RANK:], token_positions),
        ],
        axis=-1,
    ).astype(jnp.bfloat16)


def cache_send_rows(latent_vector, owner, device_count, push_cap):
    target = owner[:, 0]
    rank_index = block_ranks(target[None, :], device_count)[0]
    return (
        jnp.zeros((device_count * push_cap, latent_vector.shape[1]), jnp.bfloat16)
        .at[target * push_cap + rank_index]
        .set(latent_vector)
    )


def packed_shards(
    tokens,
    norm_gain,
    kv_weight,
    key_value_gain,
    gate_weight,
    up_weight,
    down_weight,
    expert_index,
    route_gate,
    owner,
):
    device_count = lax.axis_size("dev")
    experts_count = device_count // GROUP
    tok_rows = tokens.shape[0]
    features = tokens.shape[1]
    capacity = 2 * tok_rows * ROUTES // experts_count
    push_cap = max(2, 2 * tok_rows // device_count)
    own_index = lax.axis_index("dev")
    normed = root_mean_scale(tokens.astype(jnp.float32), norm_gain).astype(jnp.bfloat16)
    flat_experts = expert_index.reshape(1, tok_rows * ROUTES)
    slot_index = block_ranks(flat_experts, experts_count)[0]
    expert_of = flat_experts[0]
    token_of = jnp.arange(tok_rows * ROUTES, dtype=jnp.int32) // ROUTES
    position = expert_of * capacity + slot_index
    packed = (
        jnp.zeros((experts_count * capacity, features), jnp.bfloat16)
        .at[position]
        .set(normed[token_of])
    )
    copies = jnp.broadcast_to(
        packed.reshape(experts_count, 1, capacity, features),
        (experts_count, GROUP, capacity, features),
    )
    received = lax.all_to_all(
        copies.reshape(device_count * capacity, features),
        "dev",
        split_axis=0,
        concat_axis=0,
        tiled=True,
    )
    gate_part = jnp.dot(received, gate_weight, preferred_element_type=jnp.float32)
    up_part = jnp.dot(received, up_weight, preferred_element_type=jnp.float32)
    hidden = (jax.nn.silu(gate_part) * up_part).astype(jnp.bfloat16)
    for bit_number in range(LOG_GROUP):
        partner = swapped(hidden, "dev", bit_number)
        upper_half = own_index >> bit_number & 1 == 1
        hidden = jnp.where(
            upper_half,
            jnp.concatenate([partner, hidden], axis=1),
            jnp.concatenate([hidden, partner], axis=1),
        )
    outputs = jnp.dot(hidden, down_weight, preferred_element_type=jnp.float32).astype(jnp.bfloat16)
    returned = lax.all_to_all(
        outputs.reshape(device_count, capacity, outputs.shape[1]),
        "dev",
        split_axis=0,
        concat_axis=2,
        tiled=True,
    )
    result = returned.reshape(capacity, experts_count, features)
    picked = result[slot_index, expert_of]
    weighted = route_gate.reshape(tok_rows * ROUTES, 1) * picked.astype(jnp.float32)
    combined = jnp.sum(weighted.reshape(tok_rows, ROUTES, features), axis=1)
    moe_out = combined.astype(jnp.bfloat16)
    raw_latent = jnp.dot(
        normed,
        lax.all_gather(kv_weight, "dev", axis=0, tiled=True),
        preferred_element_type=jnp.float32,
    )
    send_rows = cache_send_rows(
        latent_rows(raw_latent, key_value_gain), owner, device_count, push_cap
    )
    latent_cache = lax.all_to_all(send_rows, "dev", split_axis=0, concat_axis=0, tiled=True)
    return (moe_out, latent_cache)


def entry_kernel(
    place_ref, tokens_ref, gain_ref, index_ref, route_ref, weight_ref,
    rows0_ref, rows1_ref, half_ref, sem,
):
    rows = half_ref.shape[0]
    copy = pltpu.make_async_copy(weight_ref.at[pl.ds(place_ref[1] * rows, rows)], half_ref, sem)
    copy.start()
    tok_rows, features = tokens_ref.shape
    some = rows0_ref.shape[0]
    row = lax.broadcasted_iota(jnp.int32, (SCALE_COLUMNS, tok_rows), 0)
    expert, term = row // 3, row % 3
    left = jnp.zeros((SCALE_COLUMNS, tok_rows), jnp.float32)
    for route in range(ROUTES):
        named = index_ref[route : route + 1, :] == expert
        left = jnp.where(named, route_ref[route : route + 1, :], left)
    terms = jnp.zeros((SCALE_COLUMNS, tok_rows), jnp.float32)
    for number in range(3):
        rounded = left.astype(jnp.bfloat16).astype(jnp.float32)
        terms = jnp.where(term == number, rounded, terms)
        left = left - rounded
    terms = terms.T.astype(jnp.bfloat16)
    for part, ref in enumerate((rows0_ref, rows1_ref)):
        mine = slice(part * some, (part + 1) * some)
        values = tokens_ref[mine].astype(jnp.float32)
        scale = lax.rsqrt(jnp.mean(values * values, axis=-1, keepdims=True) + eps)
        lanes = gain_ref.shape[1]
        for piece in range(gain_ref.shape[0]):
            at_piece = slice(piece * lanes, (piece + 1) * lanes)
            values = tokens_ref[mine, at_piece].astype(jnp.float32)
            ref[:, at_piece] = (values * scale * gain_ref[piece : piece + 1, :]).astype(jnp.bfloat16)
        ref[:, features:] = terms[mine]
    copy.wait()


def entry(place, tokens, gain, expert_index, route_gate, weight):
    some, features = tokens.shape[0] // 2, tokens.shape[1]
    smem, vmem, hbm = (
        pl.BlockSpec(memory_space=space) for space in (pltpu.SMEM, pltpu.VMEM, pltpu.HBM)
    )
    rows = jax.ShapeDtypeStruct((some, features + SCALE_COLUMNS), jnp.bfloat16)
    return pl.pallas_call(
        entry_kernel,
        out_shape=[
            rows,
            rows,
            jax.ShapeDtypeStruct((weight.shape[0] // 2, weight.shape[1]), weight.dtype),
        ],
        in_specs=[smem, vmem, vmem, vmem, vmem, hbm],
        out_specs=[vmem] * 3,
        scratch_shapes=[pltpu.SemaphoreType.DMA],
        cost_estimate=BRIEF,
        name="entry",
    )(place, tokens, gain.reshape(-1, 128), expert_index.T, route_gate.T, weight)


def halves_kernel(place_ref, *refs):
    count = len(refs) // 2
    copies = []
    for index in range(count):
        weight, half = refs[index], refs[count + index]
        rows = half.shape[0]
        source = weight.at[pl.ds(place_ref[1] * rows, rows)]
        copies.append(pltpu.make_async_copy(source, half, refs[-1].at[index]))
    for copy in copies:
        copy.start()
    for copy in copies:
        copy.wait()


def halves_of(place, *weights):
    shapes = [
        jax.ShapeDtypeStruct((weight.shape[0] // 2, weight.shape[1]), weight.dtype)
        for weight in weights
    ]
    return pl.pallas_call(
        halves_kernel,
        out_shape=shapes,
        in_specs=[pl.BlockSpec(memory_space=pltpu.SMEM)]
        + [pl.BlockSpec(memory_space=pltpu.HBM)] * len(weights),
        out_specs=[pl.BlockSpec(memory_space=pltpu.VMEM)] * len(weights),
        scratch_shapes=[pltpu.SemaphoreType.DMA((len(weights),))],
        cost_estimate=BRIEF,
        name="weight_halves",
    )(place, *weights)


def begin_block(refs, buf, sems, slot, k, rep):
    wholes = len(refs) - 4 if len(refs) > 4 else len(refs) % 4
    for number in range(wholes):

        @pl.when(k == number)
        def _(number=number):
            pltpu.make_async_copy(refs[number], buf.at[slot], sems.at[number]).start()

    for index in range(wholes, len(refs), 2):
        number = wholes + (index - wholes) // 2

        @pl.when(k == number)
        def _(number=number, index=index):
            half = refs[index].shape[0]
            for ref, part in ((refs[index], rep), (refs[index + 1], 1 - rep)):
                target = buf.at[slot, pl.ds(part * half, half)]
                pltpu.make_async_copy(ref, target, sems.at[number]).start()


def await_block(buf, sems, slot, k):
    pltpu.make_async_copy(buf.at[slot], buf.at[slot], sems.at[k]).wait()


def latent_kernel(place_ref, *refs):
    row_refs, kv_refs, part_refs = refs[:6], refs[6:10], refs[10:13]
    rows_buf, kv_buf, row_sems, kv_sems = refs[13:]
    place, plane = place_ref[0], place_ref[2]
    depth, piece = rows_buf.shape[1], kv_refs[0].shape[0]
    some = row_refs[0].shape[0]
    columns = pl.ds(pl.multiple_of(plane * depth, 128), depth)
    copies = [
        pltpu.make_async_copy(
            ref.at[:, columns], rows_buf.at[pl.ds(index * some, some)], row_sems.at[index]
        )
        for index, ref in enumerate(row_refs)
    ] + [
        pltpu.make_async_copy(ref, kv_buf.at[pl.ds((place ^ k) * piece, piece)], kv_sems.at[k])
        for k, ref in enumerate(kv_refs)
    ]
    for copy in copies:
        copy.start()
    for copy in copies:
        copy.wait()
    out = jnp.dot(rows_buf[...], kv_buf[...], preferred_element_type=jnp.float32)
    for index, ref in enumerate(part_refs):
        ref[...] = out[2 * index * some : 2 * (index + 1) * some].astype(jnp.bfloat16)


def latent_parts(place, rows, kv_parts):
    some = rows[0].shape[0]
    piece, width = kv_parts[0].shape
    vmem, hbm = pl.BlockSpec(memory_space=pltpu.VMEM), pl.BlockSpec(memory_space=pltpu.HBM)
    return pl.pallas_call(
        latent_kernel,
        out_shape=[jax.ShapeDtypeStruct((2 * some, width), jnp.bfloat16)] * (len(rows) // 2),
        in_specs=[pl.BlockSpec(memory_space=pltpu.SMEM)] + [hbm] * (len(rows) + len(kv_parts)),
        out_specs=[vmem] * (len(rows) // 2),
        scratch_shapes=[
            pltpu.VMEM((len(rows) * some, GROUP * piece), jnp.bfloat16),
            pltpu.VMEM((GROUP * piece, width), jnp.bfloat16),
            pltpu.SemaphoreType.DMA((len(rows),)),
            pltpu.SemaphoreType.DMA((GROUP,)),
        ],
        compiler_params=pltpu.CompilerParams(vmem_limit_bytes=VMEM_GRANT),
        cost_estimate=BRIEF,
        name="latent_parts",
    )(place, *rows, *kv_parts)


def hidden_kernel(place_ref, *refs):
    row_refs, gate_refs, up_refs, refs = refs[:7], refs[7:13], refs[13:19], refs[19:]
    down_refs, kv_refs, refs = refs[:2], refs[2:6], refs[6:]
    hidden_ref, scale_ref, latent_ref, part_refs, refs = refs[0], refs[1], refs[2], refs[3:7], refs[7:]
    rows_buf, gate_buf, up_buf, down_buf, kv_buf = refs[:5]
    row_sems, gate_sems, up_sems, down_sems, kv_sems = refs[5:]
    place, rep, plane = place_ref[0], place_ref[1], place_ref[2]
    core = place & 1
    some = row_refs[0].shape[0]
    row_copies, first = [], 0
    for index, ref in enumerate(row_refs):
        target = rows_buf.at[pl.ds(first, ref.shape[0])]
        row_copies.append(pltpu.make_async_copy(ref, target, row_sems.at[index]))
        first += ref.shape[0]
    piece = kv_refs[0].shape[0]
    kv_copies = [
        pltpu.make_async_copy(ref, kv_buf.at[pl.ds((place ^ k) * piece, piece)], kv_sems.at[k])
        for k, ref in enumerate(kv_refs)
    ]
    for copy in row_copies:
        copy.start()
    for slot in range(GROUP):
        begin_block(gate_refs, gate_buf, gate_sems, slot, place ^ slot, rep)
        begin_block(up_refs, up_buf, up_sems, slot, place ^ slot, rep)
    for slot in range(2):
        begin_block(down_refs, down_buf, down_sems, slot, core ^ slot, rep)
    for copy in kv_copies:
        copy.start()
    for copy in row_copies:
        copy.wait()

    features, units = gate_buf.shape[1:]
    terms = rows_buf[:, features:].astype(jnp.float32)
    lane = lax.broadcasted_iota(jnp.int32, terms.shape, 1)
    own = (lane >= 3 * plane) & (lane < 3 * plane + 3)
    scale_ref[...] = jnp.sum(jnp.where(own, terms, 0.0), axis=1, keepdims=True)

    for slot in range(GROUP):
        await_block(gate_buf, gate_sems, slot, place ^ slot)
        await_block(up_buf, up_sems, slot, place ^ slot)
        rows = rows_buf[:, :features]
        gate_part = jnp.dot(rows, gate_buf[slot], preferred_element_type=jnp.float32)
        up_part = jnp.dot(rows, up_buf[slot], preferred_element_type=jnp.float32)
        hidden_ref[:, slot * units : (slot + 1) * units] = (
            gate_part / (1.0 + jnp.exp(-gate_part)) * up_part
        ).astype(jnp.bfloat16)

    for slot in range(2):
        await_block(down_buf, down_sems, slot, core ^ slot)
        weigh_block(hidden_ref, scale_ref, down_buf, slot, part_refs)

    for copy in kv_copies:
        copy.wait()
    depth = GROUP * piece
    columns = pl.ds(pl.multiple_of(plane * depth, 128), depth)
    latent = jnp.dot(
        rows_buf[4 * some : 6 * some, columns], kv_buf[...], preferred_element_type=jnp.float32
    )
    latent_ref[...] = latent.astype(jnp.bfloat16)


def weigh_block(hidden_ref, scale_ref, down_buf, slot, part_refs):
    out = jnp.dot(hidden_ref[...], down_buf[slot], preferred_element_type=jnp.float32)
    out = (out.astype(jnp.bfloat16).astype(jnp.float32) * scale_ref[...]).astype(jnp.bfloat16)
    tok_rows, width = part_refs[0].shape[0], down_buf.shape[2]
    for index, part_ref in enumerate(part_refs):
        part_ref[:, slot * width : (slot + 1) * width] = out[
            index * tok_rows : (index + 1) * tok_rows
        ]


def hidden_units(place, rows, gates, ups, near, kv_parts):
    some, extended = rows[0].shape
    features, units = gates[0].shape
    columns = near[0].shape[1]
    piece, latent_width = kv_parts[0].shape
    hbm, vmem = pl.BlockSpec(memory_space=pltpu.HBM), pl.BlockSpec(memory_space=pltpu.VMEM)
    bf16, dma = jnp.bfloat16, pltpu.SemaphoreType.DMA
    operands = (*rows, *gates, *ups, *near, *kv_parts)
    return pl.pallas_call(
        hidden_kernel,
        out_shape=[
            jax.ShapeDtypeStruct((2 * LINE * some, GROUP * units), bf16),
            jax.ShapeDtypeStruct((2 * LINE * some, 1), jnp.float32),
            jax.ShapeDtypeStruct((2 * some, latent_width), bf16),
        ]
        + [jax.ShapeDtypeStruct((2 * some, 2 * columns), bf16)] * LINE,
        in_specs=[pl.BlockSpec(memory_space=pltpu.SMEM)] + [hbm] * len(operands),
        out_specs=[vmem] * (3 + LINE),
        scratch_shapes=[
            pltpu.VMEM((2 * LINE * some, extended), bf16),
            pltpu.VMEM((GROUP, features, units), bf16),
            pltpu.VMEM((GROUP, features, units), bf16),
            pltpu.VMEM((2, GROUP * units, columns), bf16),
            pltpu.VMEM((GROUP * piece, latent_width), bf16),
            dma((len(rows),)),
            dma((GROUP,)),
            dma((GROUP,)),
            dma((2,)),
            dma((GROUP,)),
        ],
        compiler_params=pltpu.CompilerParams(vmem_limit_bytes=VMEM_GRANT),
        cost_estimate=BRIEF,
        name="hidden_units",
    )(place, *operands)


def far_kernel(place_ref, hidden_ref, scale_ref, *refs):
    down_refs, part_refs, down_buf, sems = refs[:4], refs[4:-2], refs[-2], refs[-1]
    core, rep = place_ref[0] & 1, place_ref[1]
    for slot in range(2):
        begin_block(down_refs, down_buf, sems, slot, core ^ slot, rep)
    for slot in range(2):
        await_block(down_buf, sems, slot, core ^ slot)
        weigh_block(hidden_ref, scale_ref, down_buf, slot, part_refs)


def far_products(place, hidden, scale, downs):
    tok_rows, units, width = hidden.shape[0] // LINE, hidden.shape[1], downs[0].shape[1]
    hbm, vmem = pl.BlockSpec(memory_space=pltpu.HBM), pl.BlockSpec(memory_space=pltpu.VMEM)
    return pl.pallas_call(
        far_kernel,
        out_shape=[jax.ShapeDtypeStruct((tok_rows, 2 * width), jnp.bfloat16)] * LINE,
        in_specs=[pl.BlockSpec(memory_space=pltpu.SMEM), vmem, vmem] + [hbm] * len(downs),
        out_specs=[vmem] * LINE,
        scratch_shapes=[
            pltpu.VMEM((2, units, width), jnp.bfloat16),
            pltpu.SemaphoreType.DMA((2,)),
        ],
        compiler_params=pltpu.CompilerParams(vmem_limit_bytes=VMEM_GRANT),
        cost_estimate=BRIEF,
        name="far_products",
    )(place, hidden, scale, *downs)


def dense_shards(
    tokens,
    norm_gain,
    kv_weight,
    key_value_gain,
    gate_weight,
    up_weight,
    down_weight,
    expert_index,
    route_gate,
    owner,
):
    device_count = lax.axis_size("dev")
    push_cap = max(2, 2 * tokens.shape[0] // device_count)
    own_index = lax.axis_index("dev")
    plane, place = own_index // GROUP, own_index % GROUP
    place_info = jnp.stack([place, lax.axis_index("rep"), plane]).astype(jnp.int32)
    hold = lax.optimization_barrier

    def exchange(value, distance):
        return lax.ppermute(value, "dev", [(i, i ^ distance) for i in range(device_count)])

    def across_line(value, k):
        return exchange(value, GROUP * k)

    def other_core(value):
        return exchange(value, 1)

    def other_chip(value):
        return exchange(value, 2)

    def other_rep(value):
        return lax.ppermute(value, "rep", [(0, 1), (1, 0)])

    def narrow(value):
        return value.astype(jnp.bfloat16)

    def wide(value):
        return value.astype(jnp.float32)

    gate_core, up_core = other_core(gate_weight), other_core(up_weight)
    kv_parts = tuple(exchange(kv_weight, distance) for distance in range(1, GROUP))
    rows0, rows1, gate_half = entry(
        place_info, tokens, norm_gain, expert_index, route_gate, gate_weight
    )
    rows0, gate_half, gate_core, kv_parts = hold((rows0, gate_half, gate_core, kv_parts))
    kv_parts = (kv_weight, *kv_parts)

    f0, a0 = across_line(rows0, 3), across_line(rows0, 1)
    gate_x = other_chip(gate_half)
    down_core = other_core(down_weight)
    up_half, down_half = halves_of(place_info, up_weight, down_weight)
    f0, a0, gate_x, up_core, down_core, up_half, down_half, later = hold(
        (f0, a0, gate_x, up_core, down_core, up_half, down_half, rows1)
    )

    f1, a1 = across_line(later, 3), across_line(later, 1)
    gate_y = other_rep(gate_x)
    up_x = other_chip(up_half)
    gate_x_core = other_core(gate_x)
    f0, f1, a1, gate_y, up_x, gate_x_core, down_half = hold(
        (f0, f1, a1, gate_y, up_x, gate_x_core, down_half)
    )

    c = across_line(jnp.concatenate([f0, f1]), 1)
    up_y = other_rep(up_x)
    down_x = other_chip(down_half)
    latent0, latent1, latent3 = latent_parts(
        place_info, (rows0, later, a0, a1, f0, f1), kv_parts
    )
    gate_y_core, up_x_core = other_core(gate_y), other_core(up_x)
    c, up_y, down_x, gate_y_core, up_x_core, latent1, latent3 = hold(
        (c, up_y, down_x, gate_y_core, up_x_core, latent1, latent3)
    )

    up_y_core = other_core(up_y)
    down_y, down_x_core = other_rep(down_x), other_core(down_x)
    latent1, latent3 = across_line(latent1, 1), across_line(latent3, 3)
    hidden, scale, latent2, near0, near1, near2, near3 = hidden_units(
        place_info,
        (rows0, later, a0, a1, c, f0, f1),
        (gate_weight, gate_core, gate_x, gate_y, gate_x_core, gate_y_core),
        (up_weight, up_core, up_x, up_y, up_x_core, up_y_core),
        (down_weight, down_core),
        kv_parts,
    )
    hidden, near2, latent1, latent3, down_y, down_x_core = hold(
        (hidden, near2, latent1, latent3, down_y, down_x_core)
    )
    near2_there = across_line(near2, 1)
    down_y_core = other_core(down_y)
    far0, far1, far2, far3 = far_products(
        place_info, hidden, scale, (down_x, down_y, down_x_core, down_y_core)
    )
    far2_there = across_line(far2, 1)
    near2_there, far2, latent2 = hold((near2_there, far2, latent2))
    near_sum = narrow(wide(near3) + wide(near2_there))
    near_sum, near1 = hold((near_sum, near1))
    near3_there, near1_there = across_line(near_sum, 3), across_line(near1, 1)
    latent2 = across_line(latent2, 2)
    far_sum = narrow(wide(far3) + wide(far2_there))
    far3_there, far1_there = across_line(far_sum, 3), across_line(far1, 1)
    raw_latent = wide(latent0) + wide(latent1) + wide(latent2) + wide(latent3)
    near = narrow(wide(near0) + wide(near1_there) + wide(near3_there))
    far = narrow(wide(far0) + wide(far1_there) + wide(far3_there))
    moe_out = jnp.where(
        place & 2 == 2,
        jnp.concatenate([far, near], axis=1),
        jnp.concatenate([near, far], axis=1),
    )

    send_rows = cache_send_rows(
        latent_rows(raw_latent, key_value_gain), owner, device_count, push_cap
    )
    latent_cache = lax.all_to_all(send_rows, "dev", split_axis=0, concat_axis=0, tiled=True)
    return (moe_out, latent_cache)


def solution(mesh):
    in_specs = (
        P(("rep", "dev"), None),
        P(),
        P("dev", None),
        P(),
        P(None, "dev"),
        P(None, "dev"),
        P("dev", None),
        P(("rep", "dev"), None),
        P(("rep", "dev"), None),
        P(("rep", "dev"), None),
    )
    out_specs = (P(("rep", "dev"), None), P(("rep", "dev"), None))
    dense = mesh.shape["dev"] == LINE * GROUP and mesh.shape["rep"] == 2
    shards = dense_shards if dense else packed_shards
    return jax.shard_map(shards, mesh=mesh, in_specs=in_specs, out_specs=out_specs, check_vma=False)
```

```python
import functools

import jax
import jax.numpy as jnp
from jax import lax
from jax.experimental import pallas as pl
from jax.experimental.pallas import tpu as pltpu
from jax.sharding import PartitionSpec as P

KEY_VALUE_RANK = 512
ROUTES = 2
LOG_GROUP = 2
GROUP = 4
LINE = 4
SCALE_COLUMNS = 128
MIB = 1024 * 1024
BRIEF = pl.CostEstimate(flops=1 << 20, bytes_accessed=1 << 20, transcendentals=0)


eps = 1e-06
rope_theta = 50000.0


def swapped(value, axis, stride):
    return lax.ppermute(value, axis, [(i, i ^ 1 << stride) for i in range(lax.axis_size(axis))])


def root_mean_scale(values, gain_vector):
    mean_sq = jnp.mean(values * values, axis=-1, keepdims=True)
    return values * lax.rsqrt(mean_sq + eps) * gain_vector


def apply_rotary_keys(key_part, token_positions):
    half_width = key_part.shape[-1] // 2
    frequency = rope_theta ** (
        -jnp.arange(half_width, dtype=jnp.float32) * 2.0 / key_part.shape[-1]
    )
    angles = token_positions.astype(jnp.float32)[:, None] * frequency[None, :]
    cos_part = jnp.cos(angles)
    sin_part = jnp.sin(angles)
    front_half = key_part[:, :half_width]
    back_half = key_part[:, half_width:]
    return jnp.concatenate(
        [
            front_half * cos_part - back_half * sin_part,
            back_half * cos_part + front_half * sin_part,
        ],
        axis=-1,
    )


def block_ranks(labels, label_count):
    onehot = (labels[..., None] == jnp.arange(label_count, dtype=jnp.int32)).astype(jnp.int32)
    before = jnp.cumsum(onehot, axis=1, dtype=jnp.int32) - onehot
    return jnp.sum(before * onehot, axis=-1, dtype=jnp.int32)


def latent_rows(raw_latent, key_value_gain):
    token_positions = jnp.arange(raw_latent.shape[0], dtype=jnp.int32)
    return jnp.concatenate(
        [
            root_mean_scale(raw_latent[:, :KEY_VALUE_RANK], key_value_gain),
            apply_rotary_keys(raw_latent[:, KEY_VALUE_RANK:], token_positions),
        ],
        axis=-1,
    ).astype(jnp.bfloat16)


def cache_slots(owner, device_count, push_cap):
    target = owner[:, 0]
    return target * push_cap + block_ranks(target[None, :], device_count)[0]


def cache_send_rows(latent_vector, slots, rows):
    return jnp.zeros((rows, latent_vector.shape[1]), jnp.bfloat16).at[slots].set(latent_vector)


def packed_shards(
    tokens,
    norm_gain,
    kv_weight,
    key_value_gain,
    gate_weight,
    up_weight,
    down_weight,
    expert_index,
    route_gate,
    owner,
):
    device_count = lax.axis_size("dev")
    experts_count = device_count // GROUP
    tok_rows = tokens.shape[0]
    features = tokens.shape[1]
    capacity = 2 * tok_rows * ROUTES // experts_count
    push_cap = max(2, 2 * tok_rows // device_count)
    own_index = lax.axis_index("dev")
    normed = root_mean_scale(tokens.astype(jnp.float32), norm_gain).astype(jnp.bfloat16)
    flat_experts = expert_index.reshape(1, tok_rows * ROUTES)
    slot_index = block_ranks(flat_experts, experts_count)[0]
    expert_of = flat_experts[0]
    token_of = jnp.arange(tok_rows * ROUTES, dtype=jnp.int32) // ROUTES
    position = expert_of * capacity + slot_index
    packed = (
        jnp.zeros((experts_count * capacity, features), jnp.bfloat16)
        .at[position]
        .set(normed[token_of])
    )
    copies = jnp.broadcast_to(
        packed.reshape(experts_count, 1, capacity, features),
        (experts_count, GROUP, capacity, features),
    )
    received = lax.all_to_all(
        copies.reshape(device_count * capacity, features),
        "dev",
        split_axis=0,
        concat_axis=0,
        tiled=True,
    )
    gate_part = jnp.dot(received, gate_weight, preferred_element_type=jnp.float32)
    up_part = jnp.dot(received, up_weight, preferred_element_type=jnp.float32)
    hidden = (jax.nn.silu(gate_part) * up_part).astype(jnp.bfloat16)
    for bit_number in range(LOG_GROUP):
        partner = swapped(hidden, "dev", bit_number)
        upper_half = own_index >> bit_number & 1 == 1
        hidden = jnp.where(
            upper_half,
            jnp.concatenate([partner, hidden], axis=1),
            jnp.concatenate([hidden, partner], axis=1),
        )
    outputs = jnp.dot(hidden, down_weight, preferred_element_type=jnp.float32).astype(jnp.bfloat16)
    returned = lax.all_to_all(
        outputs.reshape(device_count, capacity, outputs.shape[1]),
        "dev",
        split_axis=0,
        concat_axis=2,
        tiled=True,
    )
    result = returned.reshape(capacity, experts_count, features)
    picked = result[slot_index, expert_of]
    weighted = route_gate.reshape(tok_rows * ROUTES, 1) * picked.astype(jnp.float32)
    combined = jnp.sum(weighted.reshape(tok_rows, ROUTES, features), axis=1)
    moe_out = combined.astype(jnp.bfloat16)
    raw_latent = jnp.dot(
        normed,
        lax.all_gather(kv_weight, "dev", axis=0, tiled=True),
        preferred_element_type=jnp.float32,
    )
    send_rows = cache_send_rows(
        latent_rows(raw_latent, key_value_gain),
        cache_slots(owner, device_count, push_cap),
        device_count * push_cap,
    )
    latent_cache = lax.all_to_all(send_rows, "dev", split_axis=0, concat_axis=0, tiled=True)
    return (moe_out, latent_cache)


def entry_kernel(
    place_ref, tokens_ref, gain_ref, index_ref, route_ref, weight_ref,
    rows0_ref, rows1_ref, half_ref, sem,
):
    rows = half_ref.shape[0]
    copy = pltpu.make_async_copy(weight_ref.at[pl.ds(place_ref[1] * rows, rows)], half_ref, sem)
    copy.start()
    tok_rows, features = tokens_ref.shape
    some = rows0_ref.shape[0]
    row = lax.broadcasted_iota(jnp.int32, (SCALE_COLUMNS, tok_rows), 0)
    expert, term = row // 3, row % 3
    left = jnp.zeros((SCALE_COLUMNS, tok_rows), jnp.float32)
    for route in range(ROUTES):
        named = index_ref[route : route + 1, :] == expert
        left = jnp.where(named, route_ref[route : route + 1, :], left)
    terms = jnp.zeros((SCALE_COLUMNS, tok_rows), jnp.float32)
    for number in range(3):
        rounded = left.astype(jnp.bfloat16).astype(jnp.float32)
        terms = jnp.where(term == number, rounded, terms)
        left = left - rounded
    terms = terms.T.astype(jnp.bfloat16)
    for part, ref in enumerate((rows0_ref, rows1_ref)):
        mine = slice(part * some, (part + 1) * some)
        values = tokens_ref[mine].astype(jnp.float32)
        scale = lax.rsqrt(jnp.mean(values * values, axis=-1, keepdims=True) + eps)
        lanes = gain_ref.shape[1]
        for piece in range(gain_ref.shape[0]):
            at_piece = slice(piece * lanes, (piece + 1) * lanes)
            values = tokens_ref[mine, at_piece].astype(jnp.float32)
            ref[:, at_piece] = (values * scale * gain_ref[piece : piece + 1, :]).astype(jnp.bfloat16)
        ref[:, features:] = terms[mine]
    copy.wait()


def entry(place, tokens, gain, expert_index, route_gate, weight):
    some, features = tokens.shape[0] // 2, tokens.shape[1]
    smem, vmem, hbm = (
        pl.BlockSpec(memory_space=space) for space in (pltpu.SMEM, pltpu.VMEM, pltpu.HBM)
    )
    rows = pltpu.VMEM((some, features + SCALE_COLUMNS), jnp.bfloat16)
    return pl.pallas_call(
        entry_kernel,
        out_shape=[
            rows,
            rows,
            pltpu.VMEM((weight.shape[0] // 2, weight.shape[1]), weight.dtype),
        ],
        in_specs=[smem, vmem, vmem, vmem, vmem, hbm],
        out_specs=[vmem] * 3,
        scratch_shapes=[pltpu.SemaphoreType.DMA],
        cost_estimate=BRIEF,
        name="entry",
    )(place, tokens, gain.reshape(-1, 128), expert_index.T, route_gate.T, weight)


def halves_kernel(place_ref, *refs):
    count = len(refs) // 2
    copies = []
    for index in range(count):
        weight, half = refs[index], refs[count + index]
        rows = half.shape[0]
        source = weight.at[pl.ds(place_ref[1] * rows, rows)]
        copies.append(pltpu.make_async_copy(source, half, refs[-1].at[index]))
    for copy in copies:
        copy.start()
    for copy in copies:
        copy.wait()


def halves_of(place, *weights):
    shapes = [
        pltpu.VMEM((weight.shape[0] // 2, weight.shape[1]), weight.dtype)
        for weight in weights
    ]
    return pl.pallas_call(
        halves_kernel,
        out_shape=shapes,
        in_specs=[pl.BlockSpec(memory_space=pltpu.SMEM)]
        + [pl.BlockSpec(memory_space=pltpu.HBM)] * len(weights),
        out_specs=[pl.BlockSpec(memory_space=pltpu.VMEM)] * len(weights),
        scratch_shapes=[pltpu.SemaphoreType.DMA((len(weights),))],
        cost_estimate=BRIEF,
        name="weight_halves",
    )(place, *weights)


def begin_block(refs, buf, sems, slot, k, rep):
    wholes = len(refs) - 4 if len(refs) > 4 else len(refs) % 4
    for number in range(wholes):

        @pl.when(k == number)
        def _(number=number):
            pltpu.make_async_copy(refs[number], buf.at[slot], sems.at[number]).start()

    for index in range(wholes, len(refs), 2):
        number = wholes + (index - wholes) // 2

        @pl.when(k == number)
        def _(number=number, index=index):
            half = refs[index].shape[0]
            for ref, part in ((refs[index], rep), (refs[index + 1], 1 - rep)):
                target = buf.at[slot, pl.ds(part * half, half)]
                pltpu.make_async_copy(ref, target, sems.at[number]).start()


def await_block(buf, sems, slot, k):
    pltpu.make_async_copy(buf.at[slot], buf.at[slot], sems.at[k]).wait()


def latent_kernel(count, place_ref, *refs):
    row_refs, kv_refs, part_refs = refs[:count], refs[count : count + 4], refs[count + 4 : -4]
    rows_buf, kv_buf, row_sems, kv_sems = refs[-4:]
    place, plane = place_ref[0], place_ref[2]
    depth, piece = rows_buf.shape[1], kv_refs[0].shape[0]
    some = row_refs[0].shape[0]
    columns = pl.ds(pl.multiple_of(plane * depth, 128), depth)
    copies = [
        pltpu.make_async_copy(
            ref.at[:, columns], rows_buf.at[pl.ds(index * some, some)], row_sems.at[index]
        )
        for index, ref in enumerate(row_refs)
    ] + [
        pltpu.make_async_copy(ref, kv_buf.at[pl.ds((place ^ k) * piece, piece)], kv_sems.at[k])
        for k, ref in enumerate(kv_refs)
    ]
    for copy in copies:
        copy.start()
    for copy in copies:
        copy.wait()
    out = jnp.dot(rows_buf[...], kv_buf[...], preferred_element_type=jnp.float32)
    tok_rows = part_refs[0].shape[0]
    for index, ref in enumerate(part_refs):
        ref[...] = out[index * tok_rows : (index + 1) * tok_rows].astype(jnp.bfloat16)


def latent_parts(place, rows, kv_parts, tok_rows):
    height = sum(each.shape[0] for each in rows)
    piece, width = kv_parts[0].shape
    vmem, anywhere = pl.BlockSpec(memory_space=pltpu.VMEM), pl.BlockSpec(memory_space=pl.ANY)
    return pl.pallas_call(
        functools.partial(latent_kernel, len(rows)),
        out_shape=[pltpu.VMEM((tok_rows, width), jnp.bfloat16)] * (height // tok_rows),
        in_specs=[pl.BlockSpec(memory_space=pltpu.SMEM)]
        + [anywhere] * (len(rows) + len(kv_parts)),
        out_specs=[vmem] * (height // tok_rows),
        scratch_shapes=[
            pltpu.VMEM((height, GROUP * piece), jnp.bfloat16),
            pltpu.VMEM((GROUP * piece, width), jnp.bfloat16),
            pltpu.SemaphoreType.DMA((len(rows),)),
            pltpu.SemaphoreType.DMA((GROUP,)),
        ],
        compiler_params=pltpu.CompilerParams(vmem_limit_bytes=8 * MIB),
        cost_estimate=BRIEF,
        name="latent_parts",
    )(place, *rows, *kv_parts)


def hidden_kernel(place_ref, *refs):
    row_refs, gate_refs, up_refs, refs = refs[:7], refs[7:13], refs[13:19], refs[19:]
    down_refs, (hidden_ref, scale_ref, part_ref), refs = refs[:2], refs[2:5], refs[5:]
    rows_buf, gate_buf, up_buf, down_buf = refs[:4]
    row_sems, gate_sems, up_sems, down_sems = refs[4:]
    place, rep, plane = place_ref[0], place_ref[1], place_ref[2]
    core = place & 1
    some = row_refs[0].shape[0]
    row_copies, first = [], 0
    for index, ref in enumerate(row_refs):
        target = rows_buf.at[pl.ds(first, ref.shape[0])]
        row_copies.append(pltpu.make_async_copy(ref, target, row_sems.at[index]))
        first += ref.shape[0]

    def begin_slot(slot):
        begin_block(gate_refs, gate_buf, gate_sems, slot, place ^ slot, rep)
        begin_block(up_refs, up_buf, up_sems, slot, place ^ slot, rep)

    for copy in row_copies:
        copy.start()
    begin_slot(0)
    for copy in row_copies:
        copy.wait()
    begin_slot(1)

    features, units = gate_buf.shape[1:]
    terms = rows_buf[:, features:].astype(jnp.float32)
    lane = lax.broadcasted_iota(jnp.int32, terms.shape, 1)
    own = (lane >= 3 * plane) & (lane < 3 * plane + 3)
    scale_ref[...] = jnp.sum(jnp.where(own, terms, 0.0), axis=1, keepdims=True)

    for slot in range(GROUP):
        await_block(gate_buf, gate_sems, slot, place ^ slot)
        await_block(up_buf, up_sems, slot, place ^ slot)
        if slot + 2 < GROUP:
            begin_slot(slot + 2)
        else:
            begin_block(down_refs, down_buf, down_sems, slot - 2, core ^ (slot - 2), rep)
        rows = rows_buf[:, :features]
        gate_part = jnp.dot(rows, gate_buf[slot], preferred_element_type=jnp.float32)
        up_part = jnp.dot(rows, up_buf[slot], preferred_element_type=jnp.float32)
        hidden_ref[:, slot * units : (slot + 1) * units] = (
            gate_part / (1.0 + jnp.exp(-gate_part)) * up_part
        ).astype(jnp.bfloat16)

    for slot in range(2):
        await_block(down_buf, down_sems, slot, core ^ slot)
        width = down_buf.shape[2]
        part_ref[:, slot * width : (slot + 1) * width] = weighed(
            hidden_ref[4 * some : 6 * some], scale_ref[4 * some : 6 * some], down_buf[slot]
        )


def weighed(hidden, scale, down):
    out = jnp.dot(hidden, down, preferred_element_type=jnp.float32)
    return (out.astype(jnp.bfloat16).astype(jnp.float32) * scale).astype(jnp.bfloat16)


def hidden_units(place, rows, gates, ups, near):
    some, extended = rows[0].shape
    features, units = gates[0].shape
    columns = near[0].shape[1]
    hbm, vmem = pl.BlockSpec(memory_space=pltpu.HBM), pl.BlockSpec(memory_space=pltpu.VMEM)
    bf16, dma = jnp.bfloat16, pltpu.SemaphoreType.DMA
    operands = (*rows, *gates, *ups, *near)
    late = [rows[4], ups[3], ups[4], ups[5], gates[5]]
    specs = [
        pl.BlockSpec(memory_space=pl.ANY if any(each is one for one in late) else pltpu.HBM)
        for each in operands
    ]
    return pl.pallas_call(
        hidden_kernel,
        out_shape=[
            pltpu.VMEM((2 * LINE * some, GROUP * units), bf16),
            pltpu.VMEM((2 * LINE * some, 1), jnp.float32),
        ]
        + [pltpu.VMEM((2 * some, 2 * columns), bf16)],
        in_specs=[pl.BlockSpec(memory_space=pltpu.SMEM)] + specs,
        out_specs=[vmem] * 3,
        scratch_shapes=[
            pltpu.VMEM((2 * LINE * some, extended), bf16),
            pltpu.VMEM((GROUP, features, units), bf16),
            pltpu.VMEM((GROUP, features, units), bf16),
            pltpu.VMEM((2, GROUP * units, columns), bf16),
            dma((len(rows),)),
            dma((GROUP,)),
            dma((GROUP,)),
            dma((2,)),
        ],
        compiler_params=pltpu.CompilerParams(vmem_limit_bytes=52 * MIB),
        cost_estimate=BRIEF,
        name="hidden_units",
    )(place, *operands)


def rest_kernel(place_ref, hidden_ref, scale_ref, *refs):
    down_refs, (part0_ref, part1_ref, part3_ref, far_ref), (down_buf, sems) = refs[:6], refs[6:10], refs[10:]
    place, rep = place_ref[0], place_ref[1]

    def begin_slot(slot):
        begin_block(down_refs, down_buf, sems, slot, place ^ slot, rep)

    begin_slot(0)
    begin_slot(1)
    tok_rows, width = part0_ref.shape[0], down_buf.shape[2]
    for slot in range(GROUP):
        await_block(down_buf, sems, slot, place ^ slot)
        if slot + 2 < GROUP:
            begin_slot(slot + 2)
        out = weighed(hidden_ref[...], scale_ref[...], down_buf[slot])
        columns = slice(slot * width, (slot + 1) * width)
        for k, ref in ((0, part0_ref), (1, part1_ref), (3, part3_ref)):
            ref[:, columns] = out[k * tok_rows : (k + 1) * tok_rows]

        @pl.when((place ^ slot) >= 2)
        def _(slot=slot, out=out):
            columns = slice((slot % 2) * width, (slot % 2 + 1) * width)
            far_ref[:, columns] = out[2 * tok_rows : 3 * tok_rows]


def rest_products(place, hidden, scale, downs):
    tok_rows, units, width = hidden.shape[0] // LINE, hidden.shape[1], downs[0].shape[1]
    hbm, vmem = pl.BlockSpec(memory_space=pltpu.HBM), pl.BlockSpec(memory_space=pltpu.VMEM)
    return pl.pallas_call(
        rest_kernel,
        out_shape=[pltpu.VMEM((tok_rows, GROUP * width), jnp.bfloat16)] * 3
        + [pltpu.VMEM((tok_rows, 2 * width), jnp.bfloat16)],
        in_specs=[pl.BlockSpec(memory_space=pltpu.SMEM), vmem, vmem]
        + [hbm] * (len(downs) - 1)
        + [pl.BlockSpec(memory_space=pl.ANY)],
        out_specs=[vmem] * 4,
        scratch_shapes=[
            pltpu.VMEM((GROUP, units, width), jnp.bfloat16),
            pltpu.SemaphoreType.DMA((GROUP,)),
        ],
        compiler_params=pltpu.CompilerParams(vmem_limit_bytes=40 * MIB),
        cost_estimate=BRIEF,
        name="rest_products",
    )(place, hidden, scale, *downs)


def order_kernel(place_ref, blocks_ref, ordered_ref, sems):
    plane, chip, core = place_ref[0], place_ref[1], place_ref[2]
    count = sems.shape[0]
    rows = ordered_ref.shape[0] // count
    copies = []
    for source in range(count):
        far = ((source & 1) ^ core) * (count // 2) + ((source >> 1 & 1) ^ chip) * (count // 4)
        block = far + ((source >> 2) ^ plane)
        copies.append(
            pltpu.make_async_copy(
                blocks_ref.at[pl.ds(block * rows, rows)],
                ordered_ref.at[pl.ds(source * rows, rows)],
                sems.at[source],
            )
        )
    for copy in copies:
        copy.start()
    for copy in copies:
        copy.wait()


def in_source_order(place, blocks, rows):
    return pl.pallas_call(
        order_kernel,
        out_shape=jax.ShapeDtypeStruct(blocks.shape, blocks.dtype),
        in_specs=[
            pl.BlockSpec(memory_space=pltpu.SMEM),
            pl.BlockSpec(memory_space=pl.ANY),
        ],
        out_specs=pl.BlockSpec(memory_space=pltpu.VMEM),
        scratch_shapes=[pltpu.SemaphoreType.DMA((blocks.shape[0] // rows,))],
        cost_estimate=BRIEF,
        name="in_source_order",
    )(place, blocks)


def dense_shards(
    tokens,
    norm_gain,
    kv_weight,
    key_value_gain,
    gate_weight,
    up_weight,
    down_weight,
    expert_index,
    route_gate,
    owner,
):
    device_count = lax.axis_size("dev")
    push_cap = max(2, 2 * tokens.shape[0] // device_count)
    own_index = lax.axis_index("dev")
    plane, place = own_index // GROUP, own_index % GROUP
    place_info = jnp.stack([place, lax.axis_index("rep"), plane]).astype(jnp.int32)
    hold = lax.optimization_barrier

    def exchange(value, distance):
        return lax.ppermute(value, "dev", [(i, i ^ distance) for i in range(device_count)])

    def across_line(value, k):
        return exchange(value, GROUP * k)

    def other_core(value):
        return exchange(value, 1)

    def other_chip(value):
        return exchange(value, 2)

    def other_rep(value):
        return lax.ppermute(value, "rep", [(0, 1), (1, 0)])

    def narrow(value):
        return value.astype(jnp.bfloat16)

    def wide(value):
        return value.astype(jnp.float32)

    some = tokens.shape[0] // 2
    slots = cache_slots(owner, device_count, push_cap)

    gate_core, up_core = other_core(gate_weight), other_core(up_weight)
    kv_core, kv_x = other_core(kv_weight), other_chip(kv_weight)
    rows0, rows1, gate_half = entry(
        place_info, tokens, norm_gain, expert_index, route_gate, gate_weight
    )
    rows0, rows1, gate_half, gate_core, up_core, kv_core, kv_x, up_own, down_own = hold(
        (rows0, rows1, gate_half, gate_core, up_core, kv_core, kv_x, up_weight, down_weight)
    )

    f0, a0 = across_line(rows0, 3), across_line(rows0, 1)
    gate_x = other_chip(gate_half)
    down_core, kv_x_core = other_core(down_own), other_core(kv_x)
    up_half, down_half = halves_of(place_info, up_own, down_own)
    f0, a0, gate_x, down_core, kv_x_core, up_half, down_half, later, slots = hold(
        (f0, a0, gate_x, down_core, kv_x_core, up_half, down_half, rows1, slots)
    )
    kv_parts = (kv_weight, kv_core, kv_x, kv_x_core)

    f1, a1 = across_line(later, 3), across_line(later, 1)
    gate_y = other_rep(gate_x)
    up_x = other_chip(up_half)
    gate_x_core = other_core(gate_x)
    f0, f1, a1, gate_y, up_x, gate_x_core, down_half = hold(
        (f0, f1, a1, gate_y, up_x, gate_x_core, down_half)
    )

    c = across_line(jnp.concatenate([f0, f1]), 1)
    up_y = other_rep(up_x)
    down_x = other_chip(down_half)
    latent0, latent1, latent3 = latent_parts(
        place_info, (rows0, later, a0, a1, f0, f1), kv_parts, 2 * some
    )
    gate_y_core, up_x_core = other_core(gate_y), other_core(up_x)
    c, up_y, down_x, gate_y_core, up_x_core, latent1, latent3 = hold(
        (c, up_y, down_x, gate_y_core, up_x_core, latent1, latent3)
    )

    up_y_core = other_core(up_y)
    down_y, down_x_core = other_rep(down_x), other_core(down_x)
    (latent2,) = latent_parts(place_info, (c,), kv_parts, 2 * some)
    latents = [across_line(value, k) for k, value in ((1, latent1), (2, latent2), (3, latent3))]
    hidden, scale, near2 = hidden_units(
        place_info,
        (rows0, later, a0, a1, c, f0, f1),
        (gate_weight, gate_core, gate_x, gate_y, gate_x_core, gate_y_core),
        (up_weight, up_core, up_x, up_y, up_x_core, up_y_core),
        (down_weight, down_core),
    )
    hidden, near2, latents, down_y, down_x_core = hold(
        (hidden, near2, latents, down_y, down_x_core)
    )
    near2_there = across_line(near2, 1)
    down_y_core = other_core(down_y)
    part0, part1, part3, far2 = rest_products(
        place_info,
        hidden,
        scale,
        (down_weight, down_core, down_x, down_y, down_x_core, down_y_core),
    )
    far2_there = across_line(far2, 1)

    raw_latent = wide(latent0) + sum(wide(value) for value in latents)
    send_rows = cache_send_rows(
        latent_rows(raw_latent, key_value_gain), slots, device_count * push_cap
    )
    by_plane = send_rows.reshape(LINE, GROUP, push_cap, send_rows.shape[1])

    def for_plane(number):
        return lax.dynamic_index_in_dim(by_plane, number, 0, keepdims=False)

    there = [for_plane(plane)] + [across_line(for_plane(plane ^ k), k) for k in range(1, LINE)]

    part2_there = jnp.where(
        place & 2 == 2,
        jnp.concatenate([far2_there, near2_there], axis=1),
        jnp.concatenate([near2_there, far2_there], axis=1),
    )
    part2_there, there = hold((part2_there, there))
    part_sum = narrow(wide(part3) + wide(part2_there))
    part_sum, part1 = hold((part_sum, part1))
    there3, there1 = across_line(part_sum, 3), across_line(part1, 1)

    chip, core = place >> 1, place & 1
    by_chip = jnp.stack(there).reshape(LINE, 2, 2, push_cap, send_rows.shape[1])

    def for_chip(number):
        return lax.dynamic_index_in_dim(by_chip, number, 1, keepdims=False)

    by_core = jnp.stack([for_chip(chip), other_chip(for_chip(1 - chip))])

    def for_core(number):
        return lax.dynamic_index_in_dim(by_core, number, 2, keepdims=False)

    by_source = jnp.stack([for_core(core), other_core(for_core(1 - core))])
    latent_cache = in_source_order(
        jnp.stack([plane, chip, core]).astype(jnp.int32),
        by_source.reshape(device_count * push_cap, -1),
        push_cap,
    )
    moe_out = narrow(wide(part0) + wide(there1) + wide(there3))
    return (moe_out, latent_cache)


def solution(mesh):
    in_specs = (
        P(("rep", "dev"), None),
        P(),
        P("dev", None),
        P(),
        P(None, "dev"),
        P(None, "dev"),
        P("dev", None),
        P(("rep", "dev"), None),
        P(("rep", "dev"), None),
        P(("rep", "dev"), None),
    )
    out_specs = (P(("rep", "dev"), None), P(("rep", "dev"), None))
    dense = mesh.shape["dev"] == LINE * GROUP and mesh.shape["rep"] == 2
    shards = dense_shards if dense else packed_shards
    return jax.shard_map(shards, mesh=mesh, in_specs=in_specs, out_specs=out_specs, check_vma=False)
```

```python
import functools

import jax
import jax.numpy as jnp
from jax import lax
from jax.experimental import pallas as pl
from jax.experimental.pallas import tpu as pltpu
from jax.sharding import PartitionSpec as P

KEY_VALUE_RANK = 512
ROUTES = 2
LOG_GROUP = 2
GROUP = 4
LINE = 4
SCALE_COLUMNS = 128
MIB = 1024 * 1024
BRIEF = pl.CostEstimate(flops=1 << 20, bytes_accessed=1 << 20, transcendentals=0)


eps = 1e-06
rope_theta = 50000.0


def swapped(value, axis, stride):
    return lax.ppermute(value, axis, [(i, i ^ 1 << stride) for i in range(lax.axis_size(axis))])


def root_mean_scale(values, gain_vector):
    mean_sq = jnp.mean(values * values, axis=-1, keepdims=True)
    return values * lax.rsqrt(mean_sq + eps) * gain_vector


def apply_rotary_keys(key_part, token_positions):
    half_width = key_part.shape[-1] // 2
    frequency = rope_theta ** (
        -jnp.arange(half_width, dtype=jnp.float32) * 2.0 / key_part.shape[-1]
    )
    angles = token_positions.astype(jnp.float32)[:, None] * frequency[None, :]
    cos_part = jnp.cos(angles)
    sin_part = jnp.sin(angles)
    front_half = key_part[:, :half_width]
    back_half = key_part[:, half_width:]
    return jnp.concatenate(
        [
            front_half * cos_part - back_half * sin_part,
            back_half * cos_part + front_half * sin_part,
        ],
        axis=-1,
    )


def block_ranks(labels, label_count):
    onehot = (labels[..., None] == jnp.arange(label_count, dtype=jnp.int32)).astype(jnp.int32)
    before = jnp.cumsum(onehot, axis=1, dtype=jnp.int32) - onehot
    return jnp.sum(before * onehot, axis=-1, dtype=jnp.int32)


def latent_rows(raw_latent, key_value_gain):
    token_positions = jnp.arange(raw_latent.shape[0], dtype=jnp.int32)
    return jnp.concatenate(
        [
            root_mean_scale(raw_latent[:, :KEY_VALUE_RANK], key_value_gain),
            apply_rotary_keys(raw_latent[:, KEY_VALUE_RANK:], token_positions),
        ],
        axis=-1,
    ).astype(jnp.bfloat16)


def cache_slots(owner, device_count, push_cap):
    target = owner[:, 0]
    return target * push_cap + block_ranks(target[None, :], device_count)[0]


def cache_send_rows(latent_vector, slots, rows):
    return jnp.zeros((rows, latent_vector.shape[1]), jnp.bfloat16).at[slots].set(latent_vector)


def packed_shards(
    tokens,
    norm_gain,
    kv_weight,
    key_value_gain,
    gate_weight,
    up_weight,
    down_weight,
    expert_index,
    route_gate,
    owner,
):
    device_count = lax.axis_size("dev")
    experts_count = device_count // GROUP
    tok_rows = tokens.shape[0]
    features = tokens.shape[1]
    capacity = 2 * tok_rows * ROUTES // experts_count
    push_cap = max(2, 2 * tok_rows // device_count)
    own_index = lax.axis_index("dev")
    normed = root_mean_scale(tokens.astype(jnp.float32), norm_gain).astype(jnp.bfloat16)
    flat_experts = expert_index.reshape(1, tok_rows * ROUTES)
    slot_index = block_ranks(flat_experts, experts_count)[0]
    expert_of = flat_experts[0]
    token_of = jnp.arange(tok_rows * ROUTES, dtype=jnp.int32) // ROUTES
    position = expert_of * capacity + slot_index
    packed = (
        jnp.zeros((experts_count * capacity, features), jnp.bfloat16)
        .at[position]
        .set(normed[token_of])
    )
    copies = jnp.broadcast_to(
        packed.reshape(experts_count, 1, capacity, features),
        (experts_count, GROUP, capacity, features),
    )
    received = lax.all_to_all(
        copies.reshape(device_count * capacity, features),
        "dev",
        split_axis=0,
        concat_axis=0,
        tiled=True,
    )
    gate_part = jnp.dot(received, gate_weight, preferred_element_type=jnp.float32)
    up_part = jnp.dot(received, up_weight, preferred_element_type=jnp.float32)
    hidden = (jax.nn.silu(gate_part) * up_part).astype(jnp.bfloat16)
    for bit_number in range(LOG_GROUP):
        partner = swapped(hidden, "dev", bit_number)
        upper_half = own_index >> bit_number & 1 == 1
        hidden = jnp.where(
            upper_half,
            jnp.concatenate([partner, hidden], axis=1),
            jnp.concatenate([hidden, partner], axis=1),
        )
    outputs = jnp.dot(hidden, down_weight, preferred_element_type=jnp.float32).astype(jnp.bfloat16)
    returned = lax.all_to_all(
        outputs.reshape(device_count, capacity, outputs.shape[1]),
        "dev",
        split_axis=0,
        concat_axis=2,
        tiled=True,
    )
    result = returned.reshape(capacity, experts_count, features)
    picked = result[slot_index, expert_of]
    weighted = route_gate.reshape(tok_rows * ROUTES, 1) * picked.astype(jnp.float32)
    combined = jnp.sum(weighted.reshape(tok_rows, ROUTES, features), axis=1)
    moe_out = combined.astype(jnp.bfloat16)
    raw_latent = jnp.dot(
        normed,
        lax.all_gather(kv_weight, "dev", axis=0, tiled=True),
        preferred_element_type=jnp.float32,
    )
    send_rows = cache_send_rows(
        latent_rows(raw_latent, key_value_gain),
        cache_slots(owner, device_count, push_cap),
        device_count * push_cap,
    )
    latent_cache = lax.all_to_all(send_rows, "dev", split_axis=0, concat_axis=0, tiled=True)
    return (moe_out, latent_cache)


def entry_kernel(
    place_ref, tokens_ref, gain_ref, index_ref, route_ref, weight_ref, rows_ref, half_ref, sem
):
    rows = half_ref.shape[0]
    copy = pltpu.make_async_copy(weight_ref.at[pl.ds(place_ref[1] * rows, rows)], half_ref, sem)
    copy.start()
    tok_rows, features = tokens_ref.shape
    some = tok_rows // 2
    row = lax.broadcasted_iota(jnp.int32, (SCALE_COLUMNS, tok_rows), 0)
    expert, term = row // 3, row % 3
    left = jnp.zeros((SCALE_COLUMNS, tok_rows), jnp.float32)
    for route in range(ROUTES):
        named = index_ref[route : route + 1, :] == expert
        left = jnp.where(named, route_ref[route : route + 1, :], left)
    terms = jnp.zeros((SCALE_COLUMNS, tok_rows), jnp.float32)
    for number in range(3):
        rounded = left.astype(jnp.bfloat16).astype(jnp.float32)
        terms = jnp.where(term == number, rounded, terms)
        left = left - rounded
    terms = terms.T.astype(jnp.bfloat16)
    for part in range(2):
        mine = slice(part * some, (part + 1) * some)
        values = tokens_ref[mine].astype(jnp.float32)
        scale = lax.rsqrt(jnp.mean(values * values, axis=-1, keepdims=True) + eps)
        lanes = gain_ref.shape[1]
        for piece in range(gain_ref.shape[0]):
            at_piece = slice(piece * lanes, (piece + 1) * lanes)
            values = tokens_ref[mine, at_piece].astype(jnp.float32)
            rows_ref[mine, at_piece] = (values * scale * gain_ref[piece : piece + 1, :]).astype(jnp.bfloat16)
        rows_ref[mine, features:] = terms[mine]
    copy.wait()


def entry(place, tokens, gain, expert_index, route_gate, weight):
    tok_rows, features = tokens.shape
    smem, vmem, hbm = (
        pl.BlockSpec(memory_space=space) for space in (pltpu.SMEM, pltpu.VMEM, pltpu.HBM)
    )
    return pl.pallas_call(
        entry_kernel,
        out_shape=[
            pltpu.VMEM((tok_rows, features + SCALE_COLUMNS), jnp.bfloat16),
            pltpu.VMEM((weight.shape[0] // 2, weight.shape[1]), weight.dtype),
        ],
        in_specs=[smem, vmem, vmem, vmem, vmem, hbm],
        out_specs=[vmem] * 2,
        scratch_shapes=[pltpu.SemaphoreType.DMA],
        cost_estimate=BRIEF,
        name="entry",
    )(place, tokens, gain.reshape(-1, 128), expert_index.T, route_gate.T, weight)


def halves_kernel(place_ref, *refs):
    count = len(refs) // 2
    copies = []
    for index in range(count):
        weight, half = refs[index], refs[count + index]
        rows = half.shape[0]
        source = weight.at[pl.ds(place_ref[1] * rows, rows)]
        copies.append(pltpu.make_async_copy(source, half, refs[-1].at[index]))
    for copy in copies:
        copy.start()
    for copy in copies:
        copy.wait()


def halves_of(place, *weights):
    shapes = [
        pltpu.VMEM((weight.shape[0] // 2, weight.shape[1]), weight.dtype)
        for weight in weights
    ]
    return pl.pallas_call(
        halves_kernel,
        out_shape=shapes,
        in_specs=[pl.BlockSpec(memory_space=pltpu.SMEM)]
        + [pl.BlockSpec(memory_space=pltpu.HBM)] * len(weights),
        out_specs=[pl.BlockSpec(memory_space=pltpu.VMEM)] * len(weights),
        scratch_shapes=[pltpu.SemaphoreType.DMA((len(weights),))],
        cost_estimate=BRIEF,
        name="weight_halves",
    )(place, *weights)


def begin_block(refs, buf, sems, slot, k, rep):
    wholes = len(refs) - 4 if len(refs) > 4 else len(refs) % 4
    for number in range(wholes):

        @pl.when(k == number)
        def _(number=number):
            pltpu.make_async_copy(refs[number], buf.at[slot], sems.at[number]).start()

    for index in range(wholes, len(refs), 2):
        number = wholes + (index - wholes) // 2

        @pl.when(k == number)
        def _(number=number, index=index):
            half = refs[index].shape[0]
            for ref, part in ((refs[index], rep), (refs[index + 1], 1 - rep)):
                target = buf.at[slot, pl.ds(part * half, half)]
                pltpu.make_async_copy(ref, target, sems.at[number]).start()


def await_block(buf, sems, slot, k):
    pltpu.make_async_copy(buf.at[slot], buf.at[slot], sems.at[k]).wait()


def latent_kernel(count, place_ref, *refs):
    row_refs, kv_refs, part_refs = refs[:count], refs[count : count + 4], refs[count + 4 : -4]
    rows_buf, kv_buf, row_sems, kv_sems = refs[-4:]
    place, plane = place_ref[0], place_ref[2]
    depth, piece = rows_buf.shape[1], kv_refs[0].shape[0]
    some = row_refs[0].shape[0]
    columns = pl.ds(pl.multiple_of(plane * depth, 128), depth)
    copies = [
        pltpu.make_async_copy(
            ref.at[:, columns], rows_buf.at[pl.ds(index * some, some)], row_sems.at[index]
        )
        for index, ref in enumerate(row_refs)
    ] + [
        pltpu.make_async_copy(ref, kv_buf.at[pl.ds((place ^ k) * piece, piece)], kv_sems.at[k])
        for k, ref in enumerate(kv_refs)
    ]
    for copy in copies:
        copy.start()
    for copy in copies:
        copy.wait()
    out = jnp.dot(rows_buf[...], kv_buf[...], preferred_element_type=jnp.float32)
    tok_rows = part_refs[0].shape[0]
    for index, ref in enumerate(part_refs):
        ref[...] = out[index * tok_rows : (index + 1) * tok_rows].astype(jnp.bfloat16)


def latent_parts(place, rows, kv_parts, tok_rows):
    height = sum(each.shape[0] for each in rows)
    piece, width = kv_parts[0].shape
    vmem, anywhere = pl.BlockSpec(memory_space=pltpu.VMEM), pl.BlockSpec(memory_space=pl.ANY)
    return pl.pallas_call(
        functools.partial(latent_kernel, len(rows)),
        out_shape=[pltpu.VMEM((tok_rows, width), jnp.bfloat16)] * (height // tok_rows),
        in_specs=[pl.BlockSpec(memory_space=pltpu.SMEM)]
        + [anywhere] * (len(rows) + len(kv_parts)),
        out_specs=[vmem] * (height // tok_rows),
        scratch_shapes=[
            pltpu.VMEM((height, GROUP * piece), jnp.bfloat16),
            pltpu.VMEM((GROUP * piece, width), jnp.bfloat16),
            pltpu.SemaphoreType.DMA((len(rows),)),
            pltpu.SemaphoreType.DMA((GROUP,)),
        ],
        compiler_params=pltpu.CompilerParams(vmem_limit_bytes=8 * MIB),
        cost_estimate=BRIEF,
        name="latent_parts",
    )(place, *rows, *kv_parts)


def hidden_kernel(place_ref, *refs):
    row_refs, gate_refs, up_refs, refs = refs[:4], refs[4:10], refs[10:16], refs[16:]
    down_refs, (hidden_ref, scale_ref, part_ref), refs = refs[:2], refs[2:5], refs[5:]
    rows_buf, gate_buf, up_buf, down_buf = refs[:4]
    row_sems, gate_sems, up_sems, down_sems = refs[4:]
    place, rep, plane = place_ref[0], place_ref[1], place_ref[2]
    core = place & 1
    tok_rows = row_refs[0].shape[0]
    row_copies, first = [], 0
    for index, ref in enumerate(row_refs):
        target = rows_buf.at[pl.ds(first, ref.shape[0])]
        row_copies.append(pltpu.make_async_copy(ref, target, row_sems.at[index]))
        first += ref.shape[0]

    def begin_slot(slot):
        begin_block(gate_refs, gate_buf, gate_sems, slot, place ^ slot, rep)
        begin_block(up_refs, up_buf, up_sems, slot, place ^ slot, rep)

    for copy in row_copies:
        copy.start()
    begin_slot(0)
    for copy in row_copies:
        copy.wait()
    begin_slot(1)

    features, units = gate_buf.shape[1:]
    terms = rows_buf[:, features:].astype(jnp.float32)
    lane = lax.broadcasted_iota(jnp.int32, terms.shape, 1)
    own = (lane >= 3 * plane) & (lane < 3 * plane + 3)
    scale_ref[...] = jnp.sum(jnp.where(own, terms, 0.0), axis=1, keepdims=True)

    for slot in range(GROUP):
        await_block(gate_buf, gate_sems, slot, place ^ slot)
        await_block(up_buf, up_sems, slot, place ^ slot)
        if slot + 2 < GROUP:
            begin_slot(slot + 2)
        else:
            begin_block(down_refs, down_buf, down_sems, slot - 2, core ^ (slot - 2), rep)
        rows = rows_buf[:, :features]
        gate_part = jnp.dot(rows, gate_buf[slot], preferred_element_type=jnp.float32)
        up_part = jnp.dot(rows, up_buf[slot], preferred_element_type=jnp.float32)
        hidden_ref[:, slot * units : (slot + 1) * units] = (
            gate_part / (1.0 + jnp.exp(-gate_part)) * up_part
        ).astype(jnp.bfloat16)

    for slot in range(2):
        await_block(down_buf, down_sems, slot, core ^ slot)
        width = down_buf.shape[2]
        part_ref[:, slot * width : (slot + 1) * width] = weighed(
            hidden_ref[2 * tok_rows : 3 * tok_rows],
            scale_ref[2 * tok_rows : 3 * tok_rows],
            down_buf[slot],
        )


def weighed(hidden, scale, down):
    out = jnp.dot(hidden, down, preferred_element_type=jnp.float32)
    return (out.astype(jnp.bfloat16).astype(jnp.float32) * scale).astype(jnp.bfloat16)


def hidden_units(place, rows, gates, ups, near):
    tok_rows, extended = rows[0].shape
    features, units = gates[0].shape
    columns = near[0].shape[1]
    hbm, vmem = pl.BlockSpec(memory_space=pltpu.HBM), pl.BlockSpec(memory_space=pltpu.VMEM)
    bf16, dma = jnp.bfloat16, pltpu.SemaphoreType.DMA
    operands = (*rows, *gates, *ups, *near)
    late = [rows[2], ups[3], ups[4], ups[5], gates[5]]
    specs = [
        pl.BlockSpec(memory_space=pl.ANY if any(each is one for one in late) else pltpu.HBM)
        for each in operands
    ]
    return pl.pallas_call(
        hidden_kernel,
        out_shape=[
            pltpu.VMEM((LINE * tok_rows, GROUP * units), bf16),
            pltpu.VMEM((LINE * tok_rows, 1), jnp.float32),
        ]
        + [pltpu.VMEM((tok_rows, 2 * columns), bf16)],
        in_specs=[pl.BlockSpec(memory_space=pltpu.SMEM)] + specs,
        out_specs=[vmem] * 3,
        scratch_shapes=[
            pltpu.VMEM((LINE * tok_rows, extended), bf16),
            pltpu.VMEM((GROUP, features, units), bf16),
            pltpu.VMEM((GROUP, features, units), bf16),
            pltpu.VMEM((2, GROUP * units, columns), bf16),
            dma((len(rows),)),
            dma((GROUP,)),
            dma((GROUP,)),
            dma((2,)),
        ],
        compiler_params=pltpu.CompilerParams(vmem_limit_bytes=52 * MIB),
        cost_estimate=BRIEF,
        name="hidden_units",
    )(place, *operands)


def rest_kernel(place_ref, hidden_ref, scale_ref, *refs):
    down_refs, (part0_ref, part1_ref, part3_ref, far_ref), (down_buf, sems) = refs[:6], refs[6:10], refs[10:]
    place, rep = place_ref[0], place_ref[1]

    def begin_slot(slot):
        begin_block(down_refs, down_buf, sems, slot, place ^ slot, rep)

    begin_slot(0)
    begin_slot(1)
    tok_rows, width = part0_ref.shape[0], down_buf.shape[2]
    for slot in range(GROUP):
        await_block(down_buf, sems, slot, place ^ slot)
        if slot + 2 < GROUP:
            begin_slot(slot + 2)
        out = weighed(hidden_ref[...], scale_ref[...], down_buf[slot])
        columns = slice(slot * width, (slot + 1) * width)
        for k, ref in ((0, part0_ref), (1, part1_ref), (3, part3_ref)):
            ref[:, columns] = out[k * tok_rows : (k + 1) * tok_rows]

        @pl.when((place ^ slot) >= 2)
        def _(slot=slot, out=out):
            columns = slice((slot % 2) * width, (slot % 2 + 1) * width)
            far_ref[:, columns] = out[2 * tok_rows : 3 * tok_rows]


def rest_products(place, hidden, scale, downs):
    tok_rows, units, width = hidden.shape[0] // LINE, hidden.shape[1], downs[0].shape[1]
    hbm, vmem = pl.BlockSpec(memory_space=pltpu.HBM), pl.BlockSpec(memory_space=pltpu.VMEM)
    return pl.pallas_call(
        rest_kernel,
        out_shape=[pltpu.VMEM((tok_rows, GROUP * width), jnp.bfloat16)] * 3
        + [pltpu.VMEM((tok_rows, 2 * width), jnp.bfloat16)],
        in_specs=[pl.BlockSpec(memory_space=pltpu.SMEM), vmem, vmem]
        + [hbm] * (len(downs) - 1)
        + [pl.BlockSpec(memory_space=pl.ANY)],
        out_specs=[vmem] * 4,
        scratch_shapes=[
            pltpu.VMEM((GROUP, units, width), jnp.bfloat16),
            pltpu.SemaphoreType.DMA((GROUP,)),
        ],
        compiler_params=pltpu.CompilerParams(vmem_limit_bytes=40 * MIB),
        cost_estimate=BRIEF,
        name="rest_products",
    )(place, hidden, scale, *downs)


def order_kernel(place_ref, blocks_ref, ordered_ref, sems):
    plane, chip, core = place_ref[0], place_ref[1], place_ref[2]
    count = sems.shape[0]
    rows = ordered_ref.shape[0] // count
    copies = []
    for source in range(count):
        far = ((source & 1) ^ core) * (count // 2) + ((source >> 1 & 1) ^ chip) * (count // 4)
        block = far + ((source >> 2) ^ plane)
        copies.append(
            pltpu.make_async_copy(
                blocks_ref.at[pl.ds(block * rows, rows)],
                ordered_ref.at[pl.ds(source * rows, rows)],
                sems.at[source],
            )
        )
    for copy in copies:
        copy.start()
    for copy in copies:
        copy.wait()


def in_source_order(place, blocks, rows):
    return pl.pallas_call(
        order_kernel,
        out_shape=jax.ShapeDtypeStruct(blocks.shape, blocks.dtype),
        in_specs=[
            pl.BlockSpec(memory_space=pltpu.SMEM),
            pl.BlockSpec(memory_space=pl.ANY),
        ],
        out_specs=pl.BlockSpec(memory_space=pltpu.VMEM),
        scratch_shapes=[pltpu.SemaphoreType.DMA((blocks.shape[0] // rows,))],
        cost_estimate=BRIEF,
        name="in_source_order",
    )(place, blocks)


def dense_shards(
    tokens,
    norm_gain,
    kv_weight,
    key_value_gain,
    gate_weight,
    up_weight,
    down_weight,
    expert_index,
    route_gate,
    owner,
):
    device_count = lax.axis_size("dev")
    push_cap = max(2, 2 * tokens.shape[0] // device_count)
    own_index = lax.axis_index("dev")
    plane, place = own_index // GROUP, own_index % GROUP
    place_info = jnp.stack([place, lax.axis_index("rep"), plane]).astype(jnp.int32)
    hold = lax.optimization_barrier

    def exchange(value, distance):
        return lax.ppermute(value, "dev", [(i, i ^ distance) for i in range(device_count)])

    def across_line(value, k):
        return exchange(value, GROUP * k)

    def other_core(value):
        return exchange(value, 1)

    def other_chip(value):
        return exchange(value, 2)

    def other_rep(value):
        return lax.ppermute(value, "rep", [(0, 1), (1, 0)])

    def narrow(value):
        return value.astype(jnp.bfloat16)

    def wide(value):
        return value.astype(jnp.float32)

    slots = cache_slots(owner, device_count, push_cap)

    kv_core, kv_x = other_core(kv_weight), other_chip(kv_weight)
    gate_own, up_own, place_info = hold((gate_weight, up_weight, place_info))
    gate_core, up_core = other_core(gate_own), other_core(up_own)
    rows, gate_half = entry(
        place_info, tokens, norm_gain, expert_index, route_gate, gate_weight
    )
    rows, gate_half, gate_core, up_core, kv_core, kv_x, up_own, down_own = hold(
        (rows, gate_half, gate_core, up_core, kv_core, kv_x, up_weight, down_weight)
    )

    f = across_line(rows, 3)
    gate_x = other_chip(gate_half)
    down_core, kv_x_core = other_core(down_own), other_core(kv_x)
    up_half, down_half = halves_of(place_info, up_own, down_own)
    rows, up_half = hold((rows, up_half))
    a = across_line(rows, 1)
    gate_x, down_core, kv_x_core, up_half, down_half, slots = hold(
        (gate_x, down_core, kv_x_core, up_half, down_half, slots)
    )
    kv_parts = (kv_weight, kv_core, kv_x, kv_x_core)

    gate_y = other_rep(gate_x)
    up_x = other_chip(up_half)
    gate_x_core = other_core(gate_x)
    gate_y, up_x, gate_x_core, down_half = hold((gate_y, up_x, gate_x_core, down_half))

    c = across_line(f, 1)
    up_y = other_rep(up_x)
    down_x = other_chip(down_half)
    latent0, latent1, latent3 = latent_parts(
        place_info, (rows, a, f), kv_parts, tokens.shape[0]
    )
    gate_y_core, up_x_core = other_core(gate_y), other_core(up_x)
    c, up_y, down_x, gate_y_core, up_x_core, latent1, latent3 = hold(
        (c, up_y, down_x, gate_y_core, up_x_core, latent1, latent3)
    )

    up_y_core = other_core(up_y)
    down_y, down_x_core = other_rep(down_x), other_core(down_x)
    (latent2,) = latent_parts(place_info, (c,), kv_parts, tokens.shape[0])
    latents = [across_line(value, k) for k, value in ((1, latent1), (2, latent2), (3, latent3))]
    hidden, scale, near2 = hidden_units(
        place_info,
        (rows, a, c, f),
        (gate_weight, gate_core, gate_x, gate_y, gate_x_core, gate_y_core),
        (up_weight, up_core, up_x, up_y, up_x_core, up_y_core),
        (down_weight, down_core),
    )
    hidden, near2, latents, down_y, down_x_core = hold(
        (hidden, near2, latents, down_y, down_x_core)
    )
    near2_there = across_line(near2, 1)
    down_y_core = other_core(down_y)
    part0, part1, part3, far2 = rest_products(
        place_info,
        hidden,
        scale,
        (down_weight, down_core, down_x, down_y, down_x_core, down_y_core),
    )
    far2_there = across_line(far2, 1)

    raw_latent = wide(latent0) + sum(wide(value) for value in latents)
    send_rows = cache_send_rows(
        latent_rows(raw_latent, key_value_gain), slots, device_count * push_cap
    )
    by_plane = send_rows.reshape(LINE, GROUP, push_cap, send_rows.shape[1])

    def for_plane(number):
        return lax.dynamic_index_in_dim(by_plane, number, 0, keepdims=False)

    there = [for_plane(plane)] + [across_line(for_plane(plane ^ k), k) for k in range(1, LINE)]

    part2_there = jnp.where(
        place & 2 == 2,
        jnp.concatenate([far2_there, near2_there], axis=1),
        jnp.concatenate([near2_there, far2_there], axis=1),
    )
    part2_there, there = hold((part2_there, there))
    part_sum = narrow(wide(part3) + wide(part2_there))
    part_sum, part1 = hold((part_sum, part1))
    there3, there1 = across_line(part_sum, 3), across_line(part1, 1)

    chip, core = place >> 1, place & 1
    by_chip = jnp.stack(there).reshape(LINE, 2, 2, push_cap, send_rows.shape[1])

    def for_chip(number):
        return lax.dynamic_index_in_dim(by_chip, number, 1, keepdims=False)

    by_core = jnp.stack([for_chip(chip), other_chip(for_chip(1 - chip))])

    def for_core(number):
        return lax.dynamic_index_in_dim(by_core, number, 2, keepdims=False)

    by_source = jnp.stack([for_core(core), other_core(for_core(1 - core))])
    latent_cache = in_source_order(
        jnp.stack([plane, chip, core]).astype(jnp.int32),
        by_source.reshape(device_count * push_cap, -1),
        push_cap,
    )
    moe_out = narrow(wide(part0) + wide(there1) + wide(there3))
    return (moe_out, latent_cache)


def solution(mesh):
    in_specs = (
        P(("rep", "dev"), None),
        P(),
        P("dev", None),
        P(),
        P(None, "dev"),
        P(None, "dev"),
        P("dev", None),
        P(("rep", "dev"), None),
        P(("rep", "dev"), None),
        P(("rep", "dev"), None),
    )
    out_specs = (P(("rep", "dev"), None), P(("rep", "dev"), None))
    dense = mesh.shape["dev"] == LINE * GROUP and mesh.shape["rep"] == 2
    shards = dense_shards if dense else packed_shards
    return jax.shard_map(shards, mesh=mesh, in_specs=in_specs, out_specs=out_specs, check_vma=False)
```

```python
import functools

import jax
import jax.numpy as jnp
from jax import lax
from jax.experimental import pallas as pl
from jax.experimental.pallas import tpu as pltpu
from jax.sharding import PartitionSpec as P

KEY_VALUE_RANK = 512
ROUTES = 2
LOG_GROUP = 2
GROUP = 4
LINE = 4
SCALE_COLUMNS = 128
MIB = 1024 * 1024
BRIEF = pl.CostEstimate(flops=1 << 20, bytes_accessed=1 << 20, transcendentals=0)


eps = 1e-06
rope_theta = 50000.0


def swapped(value, axis, stride):
    return lax.ppermute(value, axis, [(i, i ^ 1 << stride) for i in range(lax.axis_size(axis))])


def root_mean_scale(values, gain_vector):
    mean_sq = jnp.mean(values * values, axis=-1, keepdims=True)
    return values * lax.rsqrt(mean_sq + eps) * gain_vector


def apply_rotary_keys(key_part, token_positions):
    half_width = key_part.shape[-1] // 2
    frequency = rope_theta ** (
        -jnp.arange(half_width, dtype=jnp.float32) * 2.0 / key_part.shape[-1]
    )
    angles = token_positions.astype(jnp.float32)[:, None] * frequency[None, :]
    cos_part = jnp.cos(angles)
    sin_part = jnp.sin(angles)
    front_half = key_part[:, :half_width]
    back_half = key_part[:, half_width:]
    return jnp.concatenate(
        [
            front_half * cos_part - back_half * sin_part,
            back_half * cos_part + front_half * sin_part,
        ],
        axis=-1,
    )


def block_ranks(labels, label_count):
    onehot = (labels[..., None] == jnp.arange(label_count, dtype=jnp.int32)).astype(jnp.int32)
    before = jnp.cumsum(onehot, axis=1, dtype=jnp.int32) - onehot
    return jnp.sum(before * onehot, axis=-1, dtype=jnp.int32)


def latent_rows(raw_latent, key_value_gain):
    token_positions = jnp.arange(raw_latent.shape[0], dtype=jnp.int32)
    return jnp.concatenate(
        [
            root_mean_scale(raw_latent[:, :KEY_VALUE_RANK], key_value_gain),
            apply_rotary_keys(raw_latent[:, KEY_VALUE_RANK:], token_positions),
        ],
        axis=-1,
    ).astype(jnp.bfloat16)


def cache_slots(owner, device_count, push_cap):
    target = owner[:, 0]
    return target * push_cap + block_ranks(target[None, :], device_count)[0]


def cache_send_rows(latent_vector, slots, rows):
    return jnp.zeros((rows, latent_vector.shape[1]), jnp.bfloat16).at[slots].set(latent_vector)


def packed_shards(
    tokens,
    norm_gain,
    kv_weight,
    key_value_gain,
    gate_weight,
    up_weight,
    down_weight,
    expert_index,
    route_gate,
    owner,
):
    device_count = lax.axis_size("dev")
    experts_count = device_count // GROUP
    tok_rows = tokens.shape[0]
    features = tokens.shape[1]
    capacity = 2 * tok_rows * ROUTES // experts_count
    push_cap = max(2, 2 * tok_rows // device_count)
    own_index = lax.axis_index("dev")
    normed = root_mean_scale(tokens.astype(jnp.float32), norm_gain).astype(jnp.bfloat16)
    flat_experts = expert_index.reshape(1, tok_rows * ROUTES)
    slot_index = block_ranks(flat_experts, experts_count)[0]
    expert_of = flat_experts[0]
    token_of = jnp.arange(tok_rows * ROUTES, dtype=jnp.int32) // ROUTES
    position = expert_of * capacity + slot_index
    packed = (
        jnp.zeros((experts_count * capacity, features), jnp.bfloat16)
        .at[position]
        .set(normed[token_of])
    )
    copies = jnp.broadcast_to(
        packed.reshape(experts_count, 1, capacity, features),
        (experts_count, GROUP, capacity, features),
    )
    received = lax.all_to_all(
        copies.reshape(device_count * capacity, features),
        "dev",
        split_axis=0,
        concat_axis=0,
        tiled=True,
    )
    gate_part = jnp.dot(received, gate_weight, preferred_element_type=jnp.float32)
    up_part = jnp.dot(received, up_weight, preferred_element_type=jnp.float32)
    hidden = (jax.nn.silu(gate_part) * up_part).astype(jnp.bfloat16)
    for bit_number in range(LOG_GROUP):
        partner = swapped(hidden, "dev", bit_number)
        upper_half = own_index >> bit_number & 1 == 1
        hidden = jnp.where(
            upper_half,
            jnp.concatenate([partner, hidden], axis=1),
            jnp.concatenate([hidden, partner], axis=1),
        )
    outputs = jnp.dot(hidden, down_weight, preferred_element_type=jnp.float32).astype(jnp.bfloat16)
    returned = lax.all_to_all(
        outputs.reshape(device_count, capacity, outputs.shape[1]),
        "dev",
        split_axis=0,
        concat_axis=2,
        tiled=True,
    )
    result = returned.reshape(capacity, experts_count, features)
    picked = result[slot_index, expert_of]
    weighted = route_gate.reshape(tok_rows * ROUTES, 1) * picked.astype(jnp.float32)
    combined = jnp.sum(weighted.reshape(tok_rows, ROUTES, features), axis=1)
    moe_out = combined.astype(jnp.bfloat16)
    raw_latent = jnp.dot(
        normed,
        lax.all_gather(kv_weight, "dev", axis=0, tiled=True),
        preferred_element_type=jnp.float32,
    )
    send_rows = cache_send_rows(
        latent_rows(raw_latent, key_value_gain),
        cache_slots(owner, device_count, push_cap),
        device_count * push_cap,
    )
    latent_cache = lax.all_to_all(send_rows, "dev", split_axis=0, concat_axis=0, tiled=True)
    return (moe_out, latent_cache)


def entry_kernel(
    place_ref, tokens_ref, gain_ref, index_ref, route_ref, weight_ref, rows_ref, half_ref, sem
):
    rows = half_ref.shape[0]
    copy = pltpu.make_async_copy(weight_ref.at[pl.ds(place_ref[1] * rows, rows)], half_ref, sem)
    copy.start()
    tok_rows, features = tokens_ref.shape
    some = tok_rows // 2
    row = lax.broadcasted_iota(jnp.int32, (SCALE_COLUMNS, tok_rows), 0)
    expert, term = row // 3, row % 3
    left = jnp.zeros((SCALE_COLUMNS, tok_rows), jnp.float32)
    for route in range(ROUTES):
        named = index_ref[route : route + 1, :] == expert
        left = jnp.where(named, route_ref[route : route + 1, :], left)
    terms = jnp.zeros((SCALE_COLUMNS, tok_rows), jnp.float32)
    for number in range(3):
        rounded = left.astype(jnp.bfloat16).astype(jnp.float32)
        terms = jnp.where(term == number, rounded, terms)
        left = left - rounded
    terms = terms.T.astype(jnp.bfloat16)
    for part in range(2):
        mine = slice(part * some, (part + 1) * some)
        values = tokens_ref[mine].astype(jnp.float32)
        scale = lax.rsqrt(jnp.mean(values * values, axis=-1, keepdims=True) + eps)
        lanes = gain_ref.shape[1]
        for piece in range(gain_ref.shape[0]):
            at_piece = slice(piece * lanes, (piece + 1) * lanes)
            values = tokens_ref[mine, at_piece].astype(jnp.float32)
            rows_ref[mine, at_piece] = (values * scale * gain_ref[piece : piece + 1, :]).astype(jnp.bfloat16)
        rows_ref[mine, features:] = terms[mine]
    copy.wait()


def entry(place, tokens, gain, expert_index, route_gate, weight):
    tok_rows, features = tokens.shape
    smem, vmem, hbm = (
        pl.BlockSpec(memory_space=space) for space in (pltpu.SMEM, pltpu.VMEM, pltpu.HBM)
    )
    return pl.pallas_call(
        entry_kernel,
        out_shape=[
            pltpu.VMEM((tok_rows, features + SCALE_COLUMNS), jnp.bfloat16),
            pltpu.VMEM((weight.shape[0] // 2, weight.shape[1]), weight.dtype),
        ],
        in_specs=[smem, vmem, vmem, vmem, vmem, hbm],
        out_specs=[vmem] * 2,
        scratch_shapes=[pltpu.SemaphoreType.DMA],
        cost_estimate=BRIEF,
        name="entry",
    )(place, tokens, gain.reshape(-1, 128), expert_index.T, route_gate.T, weight)


def halves_kernel(place_ref, *refs):
    count = len(refs) // 2
    copies = []
    for index in range(count):
        weight, half = refs[index], refs[count + index]
        rows = half.shape[0]
        source = weight.at[pl.ds(place_ref[1] * rows, rows)]
        copies.append(pltpu.make_async_copy(source, half, refs[-1].at[index]))
    for copy in copies:
        copy.start()
    for copy in copies:
        copy.wait()


def halves_of(place, *weights):
    shapes = [
        pltpu.VMEM((weight.shape[0] // 2, weight.shape[1]), weight.dtype)
        for weight in weights
    ]
    return pl.pallas_call(
        halves_kernel,
        out_shape=shapes,
        in_specs=[pl.BlockSpec(memory_space=pltpu.SMEM)]
        + [pl.BlockSpec(memory_space=pltpu.HBM)] * len(weights),
        out_specs=[pl.BlockSpec(memory_space=pltpu.VMEM)] * len(weights),
        scratch_shapes=[pltpu.SemaphoreType.DMA((len(weights),))],
        cost_estimate=BRIEF,
        name="weight_halves",
    )(place, *weights)


def begin_block(refs, buf, sems, slot, k, rep):
    wholes = len(refs) - 4 if len(refs) > 4 else len(refs) % 4
    for number in range(wholes):

        @pl.when(k == number)
        def _(number=number):
            pltpu.make_async_copy(refs[number], buf.at[slot], sems.at[number]).start()

    for index in range(wholes, len(refs), 2):
        number = wholes + (index - wholes) // 2

        @pl.when(k == number)
        def _(number=number, index=index):
            half = refs[index].shape[0]
            for ref, part in ((refs[index], rep), (refs[index + 1], 1 - rep)):
                target = buf.at[slot, pl.ds(part * half, half)]
                pltpu.make_async_copy(ref, target, sems.at[number]).start()


def await_block(buf, sems, slot, k):
    pltpu.make_async_copy(buf.at[slot], buf.at[slot], sems.at[k]).wait()


def latent_kernel(count, place_ref, *refs):
    row_refs, kv_refs, part_refs = refs[:count], refs[count : count + 4], refs[count + 4 : -4]
    rows_buf, kv_buf, row_sems, kv_sems = refs[-4:]
    place, plane = place_ref[0], place_ref[2]
    depth, piece = rows_buf.shape[1], kv_refs[0].shape[0]
    some = row_refs[0].shape[0]
    columns = pl.ds(pl.multiple_of(plane * depth, 128), depth)
    copies = [
        pltpu.make_async_copy(
            ref.at[:, columns], rows_buf.at[pl.ds(index * some, some)], row_sems.at[index]
        )
        for index, ref in enumerate(row_refs)
    ] + [
        pltpu.make_async_copy(ref, kv_buf.at[pl.ds((place ^ k) * piece, piece)], kv_sems.at[k])
        for k, ref in enumerate(kv_refs)
    ]
    for copy in copies:
        copy.start()
    for copy in copies:
        copy.wait()
    out = jnp.dot(rows_buf[...], kv_buf[...], preferred_element_type=jnp.float32)
    tok_rows = part_refs[0].shape[0]
    for index, ref in enumerate(part_refs):
        ref[...] = out[index * tok_rows : (index + 1) * tok_rows].astype(jnp.bfloat16)


def latent_parts(place, rows, kv_parts, tok_rows):
    height = sum(each.shape[0] for each in rows)
    piece, width = kv_parts[0].shape
    vmem, anywhere = pl.BlockSpec(memory_space=pltpu.VMEM), pl.BlockSpec(memory_space=pl.ANY)
    return pl.pallas_call(
        functools.partial(latent_kernel, len(rows)),
        out_shape=[pltpu.VMEM((tok_rows, width), jnp.bfloat16)] * (height // tok_rows),
        in_specs=[pl.BlockSpec(memory_space=pltpu.SMEM)]
        + [anywhere] * (len(rows) + len(kv_parts)),
        out_specs=[vmem] * (height // tok_rows),
        scratch_shapes=[
            pltpu.VMEM((height, GROUP * piece), jnp.bfloat16),
            pltpu.VMEM((GROUP * piece, width), jnp.bfloat16),
            pltpu.SemaphoreType.DMA((len(rows),)),
            pltpu.SemaphoreType.DMA((GROUP,)),
        ],
        compiler_params=pltpu.CompilerParams(vmem_limit_bytes=8 * MIB),
        cost_estimate=BRIEF,
        name="latent_parts",
    )(place, *rows, *kv_parts)


def hidden_kernel(place_ref, *refs):
    row_refs, gate_refs, up_refs, refs = refs[:4], refs[4:10], refs[10:16], refs[16:]
    down_refs, (hidden_ref, scale_ref, part_ref), refs = refs[:2], refs[2:5], refs[5:]
    rows_buf, gate_buf, up_buf, down_buf = refs[:4]
    row_sems, gate_sems, up_sems, down_sems = refs[4:]
    place, rep, plane = place_ref[0], place_ref[1], place_ref[2]
    core = place & 1
    tok_rows = row_refs[0].shape[0]
    row_copies, first = [], 0
    for index, ref in enumerate(row_refs):
        target = rows_buf.at[pl.ds(first, ref.shape[0])]
        row_copies.append(pltpu.make_async_copy(ref, target, row_sems.at[index]))
        first += ref.shape[0]

    def begin_slot(slot):
        begin_block(gate_refs, gate_buf, gate_sems, slot, place ^ slot, rep)
        begin_block(up_refs, up_buf, up_sems, slot, place ^ slot, rep)

    for copy in row_copies:
        copy.start()
    begin_slot(0)
    for copy in row_copies:
        copy.wait()
    begin_slot(1)

    features, units = gate_buf.shape[1:]
    terms = rows_buf[:, features:].astype(jnp.float32)
    lane = lax.broadcasted_iota(jnp.int32, terms.shape, 1)
    own = (lane >= 3 * plane) & (lane < 3 * plane + 3)
    scale_ref[...] = jnp.sum(jnp.where(own, terms, 0.0), axis=1, keepdims=True)

    for slot in range(GROUP):
        await_block(gate_buf, gate_sems, slot, place ^ slot)
        await_block(up_buf, up_sems, slot, place ^ slot)
        if slot + 2 < GROUP:
            begin_slot(slot + 2)
        else:
            begin_block(down_refs, down_buf, down_sems, slot - 2, core ^ (slot - 2), rep)
        rows = rows_buf[:, :features]
        gate_part = jnp.dot(rows, gate_buf[slot], preferred_element_type=jnp.float32)
        up_part = jnp.dot(rows, up_buf[slot], preferred_element_type=jnp.float32)
        hidden_ref[:, slot * units : (slot + 1) * units] = (
            gate_part / (1.0 + jnp.exp(-gate_part)) * up_part
        ).astype(jnp.bfloat16)

    for slot in range(2):
        await_block(down_buf, down_sems, slot, core ^ slot)
        width = down_buf.shape[2]
        part_ref[:, slot * width : (slot + 1) * width] = weighed(
            hidden_ref[2 * tok_rows : 3 * tok_rows],
            scale_ref[2 * tok_rows : 3 * tok_rows],
            down_buf[slot],
        )


def weighed(hidden, scale, down):
    out = jnp.dot(hidden, down, preferred_element_type=jnp.float32)
    return (out.astype(jnp.bfloat16).astype(jnp.float32) * scale).astype(jnp.bfloat16)


def hidden_units(place, rows, gates, ups, near):
    tok_rows, extended = rows[0].shape
    features, units = gates[0].shape
    columns = near[0].shape[1]
    hbm, vmem = pl.BlockSpec(memory_space=pltpu.HBM), pl.BlockSpec(memory_space=pltpu.VMEM)
    bf16, dma = jnp.bfloat16, pltpu.SemaphoreType.DMA
    operands = (*rows, *gates, *ups, *near)
    late = [rows[2], ups[3], ups[4], ups[5], gates[5]]
    specs = [
        pl.BlockSpec(memory_space=pl.ANY if any(each is one for one in late) else pltpu.HBM)
        for each in operands
    ]
    return pl.pallas_call(
        hidden_kernel,
        out_shape=[
            pltpu.VMEM((LINE * tok_rows, GROUP * units), bf16),
            pltpu.VMEM((LINE * tok_rows, 1), jnp.float32),
        ]
        + [pltpu.VMEM((tok_rows, 2 * columns), bf16)],
        in_specs=[pl.BlockSpec(memory_space=pltpu.SMEM)] + specs,
        out_specs=[vmem] * 3,
        scratch_shapes=[
            pltpu.VMEM((LINE * tok_rows, extended), bf16),
            pltpu.VMEM((GROUP, features, units), bf16),
            pltpu.VMEM((GROUP, features, units), bf16),
            pltpu.VMEM((2, GROUP * units, columns), bf16),
            dma((len(rows),)),
            dma((GROUP,)),
            dma((GROUP,)),
            dma((2,)),
        ],
        compiler_params=pltpu.CompilerParams(vmem_limit_bytes=52 * MIB),
        cost_estimate=BRIEF,
        name="hidden_units",
    )(place, *operands)


def rest_kernel(place_ref, hidden_ref, scale_ref, *refs):
    down_refs, (part0_ref, part1_ref, part3_ref, far_ref), (down_buf, sems) = refs[:6], refs[6:10], refs[10:]
    place, rep = place_ref[0], place_ref[1]

    def begin_slot(slot):
        begin_block(down_refs, down_buf, sems, slot, place ^ slot, rep)

    begin_slot(0)
    begin_slot(1)
    tok_rows, width = part0_ref.shape[0], down_buf.shape[2]
    for slot in range(GROUP):
        await_block(down_buf, sems, slot, place ^ slot)
        if slot + 2 < GROUP:
            begin_slot(slot + 2)
        out = weighed(hidden_ref[...], scale_ref[...], down_buf[slot])
        columns = slice(slot * width, (slot + 1) * width)
        for k, ref in ((0, part0_ref), (1, part1_ref), (3, part3_ref)):
            ref[:, columns] = out[k * tok_rows : (k + 1) * tok_rows]

        @pl.when((place ^ slot) >= 2)
        def _(slot=slot, out=out):
            columns = slice((slot % 2) * width, (slot % 2 + 1) * width)
            far_ref[:, columns] = out[2 * tok_rows : 3 * tok_rows]


def rest_products(place, hidden, scale, downs):
    tok_rows, units, width = hidden.shape[0] // LINE, hidden.shape[1], downs[0].shape[1]
    hbm, vmem = pl.BlockSpec(memory_space=pltpu.HBM), pl.BlockSpec(memory_space=pltpu.VMEM)
    return pl.pallas_call(
        rest_kernel,
        out_shape=[pltpu.VMEM((tok_rows, GROUP * width), jnp.bfloat16)] * 3
        + [pltpu.VMEM((tok_rows, 2 * width), jnp.bfloat16)],
        in_specs=[pl.BlockSpec(memory_space=pltpu.SMEM), vmem, vmem]
        + [hbm] * (len(downs) - 1)
        + [pl.BlockSpec(memory_space=pl.ANY)],
        out_specs=[vmem] * 4,
        scratch_shapes=[
            pltpu.VMEM((GROUP, units, width), jnp.bfloat16),
            pltpu.SemaphoreType.DMA((GROUP,)),
        ],
        compiler_params=pltpu.CompilerParams(vmem_limit_bytes=40 * MIB),
        cost_estimate=BRIEF,
        name="rest_products",
    )(place, hidden, scale, *downs)


def order_kernel(place_ref, blocks_ref, ordered_ref, sems):
    plane, chip, core = place_ref[0], place_ref[1], place_ref[2]
    count = sems.shape[0]
    rows = ordered_ref.shape[0] // count
    copies = []
    for source in range(count):
        far = ((source & 1) ^ core) * (count // 2) + ((source >> 1 & 1) ^ chip) * (count // 4)
        block = far + ((source >> 2) ^ plane)
        copies.append(
            pltpu.make_async_copy(
                blocks_ref.at[pl.ds(block * rows, rows)],
                ordered_ref.at[pl.ds(source * rows, rows)],
                sems.at[source],
            )
        )
    for copy in copies:
        copy.start()
    for copy in copies:
        copy.wait()


def in_source_order(place, blocks, rows):
    return pl.pallas_call(
        order_kernel,
        out_shape=jax.ShapeDtypeStruct(blocks.shape, blocks.dtype),
        in_specs=[
            pl.BlockSpec(memory_space=pltpu.SMEM),
            pl.BlockSpec(memory_space=pl.ANY),
        ],
        out_specs=pl.BlockSpec(memory_space=pltpu.VMEM),
        scratch_shapes=[pltpu.SemaphoreType.DMA((blocks.shape[0] // rows,))],
        compiler_params=pltpu.CompilerParams(vmem_limit_bytes=4 * MIB),
        cost_estimate=BRIEF,
        name="in_source_order",
    )(place, blocks)


def dense_shards(
    tokens,
    norm_gain,
    kv_weight,
    key_value_gain,
    gate_weight,
    up_weight,
    down_weight,
    expert_index,
    route_gate,
    owner,
):
    device_count = lax.axis_size("dev")
    push_cap = max(2, 2 * tokens.shape[0] // device_count)
    own_index = lax.axis_index("dev")
    plane, place = own_index // GROUP, own_index % GROUP
    place_info = jnp.stack([place, lax.axis_index("rep"), plane]).astype(jnp.int32)
    hold = lax.optimization_barrier

    def exchange(value, distance):
        return lax.ppermute(value, "dev", [(i, i ^ distance) for i in range(device_count)])

    def across_line(value, k):
        return exchange(value, GROUP * k)

    def other_core(value):
        return exchange(value, 1)

    def other_chip(value):
        return exchange(value, 2)

    def other_rep(value):
        return lax.ppermute(value, "rep", [(0, 1), (1, 0)])

    def narrow(value):
        return value.astype(jnp.bfloat16)

    def wide(value):
        return value.astype(jnp.float32)

    slots = cache_slots(owner, device_count, push_cap)

    kv_core, kv_x = other_core(kv_weight), other_chip(kv_weight)
    gate_own, up_own, place_info = hold((gate_weight, up_weight, place_info))
    gate_core, up_core = other_core(gate_own), other_core(up_own)
    rows, gate_half = entry(
        place_info, tokens, norm_gain, expert_index, route_gate, gate_weight
    )
    rows, gate_core, up_core, kv_core, kv_x, up_own, down_own = hold(
        (rows, gate_core, up_core, kv_core, kv_x, up_weight, down_weight)
    )

    f = across_line(rows, 3)
    gate_x = other_chip(gate_half)
    down_core, kv_x_core = other_core(down_own), other_core(kv_x)
    up_half, down_half = halves_of(place_info, up_own, down_own)
    rows, up_half = hold((rows, up_half))
    a = across_line(rows, 1)
    gate_x, down_core, kv_x_core, up_half, down_half, slots = hold(
        (gate_x, down_core, kv_x_core, up_half, down_half, slots)
    )
    kv_parts = (kv_weight, kv_core, kv_x, kv_x_core)

    gate_y = other_rep(gate_x)
    up_x = other_chip(up_half)
    gate_x_core = other_core(gate_x)
    gate_y, up_x, gate_x_core, down_half = hold((gate_y, up_x, gate_x_core, down_half))

    c = across_line(f, 1)
    up_y = other_rep(up_x)
    down_x = other_chip(down_half)
    latent0, latent1, latent3 = latent_parts(
        place_info, (rows, a, f), kv_parts, tokens.shape[0]
    )
    gate_y_core, up_x_core = other_core(gate_y), other_core(up_x)
    c, up_y, down_x, gate_y_core, up_x_core, latent1, latent3 = hold(
        (c, up_y, down_x, gate_y_core, up_x_core, latent1, latent3)
    )

    up_y_core = other_core(up_y)
    down_y, down_x_core = other_rep(down_x), other_core(down_x)
    (latent2,) = latent_parts(place_info, (c,), kv_parts, tokens.shape[0])
    latents = [across_line(value, k) for k, value in ((1, latent1), (2, latent2), (3, latent3))]
    hidden, scale, near2 = hidden_units(
        place_info,
        (rows, a, c, f),
        (gate_weight, gate_core, gate_x, gate_y, gate_x_core, gate_y_core),
        (up_weight, up_core, up_x, up_y, up_x_core, up_y_core),
        (down_weight, down_core),
    )
    hidden, near2, latents, down_x_core = hold((hidden, near2, latents, down_x_core))
    near2_there = across_line(near2, 1)
    hidden, down_y = hold((hidden, down_y))
    down_y_core = other_core(down_y)
    part0, part1, part3, far2 = rest_products(
        place_info,
        hidden,
        scale,
        (down_weight, down_core, down_x, down_y, down_x_core, down_y_core),
    )
    far2_there = across_line(far2, 1)

    raw_latent = wide(latent0) + sum(wide(value) for value in latents)
    send_rows = cache_send_rows(
        latent_rows(raw_latent, key_value_gain), slots, device_count * push_cap
    )
    by_plane = send_rows.reshape(LINE, GROUP, push_cap, send_rows.shape[1])

    def for_plane(number):
        return lax.dynamic_index_in_dim(by_plane, number, 0, keepdims=False)

    there = [for_plane(plane)] + [across_line(for_plane(plane ^ k), k) for k in range(1, LINE)]

    part2_there = jnp.where(
        place & 2 == 2,
        jnp.concatenate([far2_there, near2_there], axis=1),
        jnp.concatenate([near2_there, far2_there], axis=1),
    )
    part_sum = narrow(wide(part3) + wide(part2_there))
    part_sum, part1, there = hold((part_sum, part1, there))
    there3, there1 = across_line(part_sum, 3), across_line(part1, 1)

    chip, core = place >> 1, place & 1
    by_chip = jnp.stack(there).reshape(LINE, 2, 2, push_cap, send_rows.shape[1])

    def for_chip(number):
        return lax.dynamic_index_in_dim(by_chip, number, 1, keepdims=False)

    by_core = jnp.stack([for_chip(chip), other_chip(for_chip(1 - chip))])

    def for_core(number):
        return lax.dynamic_index_in_dim(by_core, number, 2, keepdims=False)

    by_source = jnp.stack([for_core(core), other_core(for_core(1 - core))])
    latent_cache = in_source_order(
        jnp.stack([plane, chip, core]).astype(jnp.int32),
        by_source.reshape(device_count * push_cap, -1),
        push_cap,
    )
    moe_out = narrow(wide(part0) + wide(there1) + wide(there3))
    return (moe_out, latent_cache)


def solution(mesh):
    in_specs = (
        P(("rep", "dev"), None),
        P(),
        P("dev", None),
        P(),
        P(None, "dev"),
        P(None, "dev"),
        P("dev", None),
        P(("rep", "dev"), None),
        P(("rep", "dev"), None),
        P(("rep", "dev"), None),
    )
    out_specs = (P(("rep", "dev"), None), P(("rep", "dev"), None))
    dense = mesh.shape["dev"] == LINE * GROUP and mesh.shape["rep"] == 2
    shards = dense_shards if dense else packed_shards
    return jax.shard_map(shards, mesh=mesh, in_specs=in_specs, out_specs=out_specs, check_vma=False)
```

```python
import functools

import jax
import jax.numpy as jnp
from jax import lax
from jax.experimental import pallas as pl
from jax.experimental.pallas import tpu as pltpu
from jax.sharding import PartitionSpec as P

KEY_VALUE_RANK = 512
ROUTES = 2
LOG_GROUP = 2
GROUP = 4
LINE = 4
SCALE_COLUMNS = 128
MIB = 1024 * 1024
BRIEF = pl.CostEstimate(flops=1 << 20, bytes_accessed=1 << 20, transcendentals=0)


eps = 1e-06
rope_theta = 50000.0


def swapped(value, axis, stride):
    return lax.ppermute(value, axis, [(i, i ^ 1 << stride) for i in range(lax.axis_size(axis))])


def root_mean_scale(values, gain_vector):
    mean_sq = jnp.mean(values * values, axis=-1, keepdims=True)
    return values * lax.rsqrt(mean_sq + eps) * gain_vector


def apply_rotary_keys(key_part, token_positions):
    half_width = key_part.shape[-1] // 2
    frequency = rope_theta ** (
        -jnp.arange(half_width, dtype=jnp.float32) * 2.0 / key_part.shape[-1]
    )
    angles = token_positions.astype(jnp.float32)[:, None] * frequency[None, :]
    cos_part = jnp.cos(angles)
    sin_part = jnp.sin(angles)
    front_half = key_part[:, :half_width]
    back_half = key_part[:, half_width:]
    return jnp.concatenate(
        [
            front_half * cos_part - back_half * sin_part,
            back_half * cos_part + front_half * sin_part,
        ],
        axis=-1,
    )


def block_ranks(labels, label_count):
    onehot = (labels[..., None] == jnp.arange(label_count, dtype=jnp.int32)).astype(jnp.int32)
    before = jnp.cumsum(onehot, axis=1, dtype=jnp.int32) - onehot
    return jnp.sum(before * onehot, axis=-1, dtype=jnp.int32)


def latent_rows(raw_latent, key_value_gain):
    token_positions = jnp.arange(raw_latent.shape[0], dtype=jnp.int32)
    return jnp.concatenate(
        [
            root_mean_scale(raw_latent[:, :KEY_VALUE_RANK], key_value_gain),
            apply_rotary_keys(raw_latent[:, KEY_VALUE_RANK:], token_positions),
        ],
        axis=-1,
    ).astype(jnp.bfloat16)


def cache_slots(owner, device_count, push_cap):
    target = owner[:, 0]
    return target * push_cap + block_ranks(target[None, :], device_count)[0]


def cache_send_rows(latent_vector, slots, rows):
    return jnp.zeros((rows, latent_vector.shape[1]), jnp.bfloat16).at[slots].set(latent_vector)


def packed_shards(
    tokens,
    norm_gain,
    kv_weight,
    key_value_gain,
    gate_weight,
    up_weight,
    down_weight,
    expert_index,
    route_gate,
    owner,
):
    device_count = lax.axis_size("dev")
    experts_count = device_count // GROUP
    tok_rows = tokens.shape[0]
    features = tokens.shape[1]
    capacity = 2 * tok_rows * ROUTES // experts_count
    push_cap = max(2, 2 * tok_rows // device_count)
    own_index = lax.axis_index("dev")
    normed = root_mean_scale(tokens.astype(jnp.float32), norm_gain).astype(jnp.bfloat16)
    flat_experts = expert_index.reshape(1, tok_rows * ROUTES)
    slot_index = block_ranks(flat_experts, experts_count)[0]
    expert_of = flat_experts[0]
    token_of = jnp.arange(tok_rows * ROUTES, dtype=jnp.int32) // ROUTES
    position = expert_of * capacity + slot_index
    packed = (
        jnp.zeros((experts_count * capacity, features), jnp.bfloat16)
        .at[position]
        .set(normed[token_of])
    )
    copies = jnp.broadcast_to(
        packed.reshape(experts_count, 1, capacity, features),
        (experts_count, GROUP, capacity, features),
    )
    received = lax.all_to_all(
        copies.reshape(device_count * capacity, features),
        "dev",
        split_axis=0,
        concat_axis=0,
        tiled=True,
    )
    gate_part = jnp.dot(received, gate_weight, preferred_element_type=jnp.float32)
    up_part = jnp.dot(received, up_weight, preferred_element_type=jnp.float32)
    hidden = (jax.nn.silu(gate_part) * up_part).astype(jnp.bfloat16)
    for bit_number in range(LOG_GROUP):
        partner = swapped(hidden, "dev", bit_number)
        upper_half = own_index >> bit_number & 1 == 1
        hidden = jnp.where(
            upper_half,
            jnp.concatenate([partner, hidden], axis=1),
            jnp.concatenate([hidden, partner], axis=1),
        )
    outputs = jnp.dot(hidden, down_weight, preferred_element_type=jnp.float32).astype(jnp.bfloat16)
    returned = lax.all_to_all(
        outputs.reshape(device_count, capacity, outputs.shape[1]),
        "dev",
        split_axis=0,
        concat_axis=2,
        tiled=True,
    )
    result = returned.reshape(capacity, experts_count, features)
    picked = result[slot_index, expert_of]
    weighted = route_gate.reshape(tok_rows * ROUTES, 1) * picked.astype(jnp.float32)
    combined = jnp.sum(weighted.reshape(tok_rows, ROUTES, features), axis=1)
    moe_out = combined.astype(jnp.bfloat16)
    raw_latent = jnp.dot(
        normed,
        lax.all_gather(kv_weight, "dev", axis=0, tiled=True),
        preferred_element_type=jnp.float32,
    )
    send_rows = cache_send_rows(
        latent_rows(raw_latent, key_value_gain),
        cache_slots(owner, device_count, push_cap),
        device_count * push_cap,
    )
    latent_cache = lax.all_to_all(send_rows, "dev", split_axis=0, concat_axis=0, tiled=True)
    return (moe_out, latent_cache)


def entry_kernel(
    place_ref, tokens_ref, gain_ref, index_ref, route_ref, weight_ref, rows_ref, half_ref, sem
):
    rows = half_ref.shape[0]
    copy = pltpu.make_async_copy(weight_ref.at[pl.ds(place_ref[1] * rows, rows)], half_ref, sem)
    copy.start()
    tok_rows, features = tokens_ref.shape
    some = tok_rows // 2
    row = lax.broadcasted_iota(jnp.int32, (SCALE_COLUMNS, tok_rows), 0)
    expert, term = row // 3, row % 3
    left = jnp.zeros((SCALE_COLUMNS, tok_rows), jnp.float32)
    for route in range(ROUTES):
        named = index_ref[route : route + 1, :] == expert
        left = jnp.where(named, route_ref[route : route + 1, :], left)
    terms = jnp.zeros((SCALE_COLUMNS, tok_rows), jnp.float32)
    for number in range(3):
        rounded = left.astype(jnp.bfloat16).astype(jnp.float32)
        terms = jnp.where(term == number, rounded, terms)
        left = left - rounded
    terms = terms.T.astype(jnp.bfloat16)
    for part in range(2):
        mine = slice(part * some, (part + 1) * some)
        values = tokens_ref[mine].astype(jnp.float32)
        scale = lax.rsqrt(jnp.mean(values * values, axis=-1, keepdims=True) + eps)
        lanes = gain_ref.shape[1]
        for piece in range(gain_ref.shape[0]):
            at_piece = slice(piece * lanes, (piece + 1) * lanes)
            values = tokens_ref[mine, at_piece].astype(jnp.float32)
            rows_ref[mine, at_piece] = (values * scale * gain_ref[piece : piece + 1, :]).astype(jnp.bfloat16)
        rows_ref[mine, features:] = terms[mine]
    copy.wait()


def entry(place, tokens, gain, expert_index, route_gate, weight):
    tok_rows, features = tokens.shape
    smem, vmem, hbm = (
        pl.BlockSpec(memory_space=space) for space in (pltpu.SMEM, pltpu.VMEM, pltpu.HBM)
    )
    return pl.pallas_call(
        entry_kernel,
        out_shape=[
            pltpu.VMEM((tok_rows, features + SCALE_COLUMNS), jnp.bfloat16),
            pltpu.VMEM((weight.shape[0] // 2, weight.shape[1]), weight.dtype),
        ],
        in_specs=[smem, vmem, vmem, vmem, vmem, hbm],
        out_specs=[vmem] * 2,
        scratch_shapes=[pltpu.SemaphoreType.DMA],
        cost_estimate=BRIEF,
        name="entry",
    )(place, tokens, gain.reshape(-1, 128), expert_index.T, route_gate.T, weight)


def halves_kernel(place_ref, *refs):
    count = len(refs) // 2
    copies = []
    for index in range(count):
        weight, half = refs[index], refs[count + index]
        rows = half.shape[0]
        source = weight.at[pl.ds(place_ref[1] * rows, rows)]
        copies.append(pltpu.make_async_copy(source, half, refs[-1].at[index]))
    for copy in copies:
        copy.start()
    for copy in copies:
        copy.wait()


def halves_of(place, *weights):
    shapes = [
        pltpu.VMEM((weight.shape[0] // 2, weight.shape[1]), weight.dtype)
        for weight in weights
    ]
    return pl.pallas_call(
        halves_kernel,
        out_shape=shapes,
        in_specs=[pl.BlockSpec(memory_space=pltpu.SMEM)]
        + [pl.BlockSpec(memory_space=pltpu.HBM)] * len(weights),
        out_specs=[pl.BlockSpec(memory_space=pltpu.VMEM)] * len(weights),
        scratch_shapes=[pltpu.SemaphoreType.DMA((len(weights),))],
        cost_estimate=BRIEF,
        name="weight_halves",
    )(place, *weights)


def begin_block(refs, buf, sems, slot, k, rep):
    wholes = len(refs) - 4 if len(refs) > 4 else len(refs) % 4
    for number in range(wholes):

        @pl.when(k == number)
        def _(number=number):
            pltpu.make_async_copy(refs[number], buf.at[slot], sems.at[number]).start()

    for index in range(wholes, len(refs), 2):
        number = wholes + (index - wholes) // 2

        @pl.when(k == number)
        def _(number=number, index=index):
            half = refs[index].shape[0]
            for ref, part in ((refs[index], rep), (refs[index + 1], 1 - rep)):
                target = buf.at[slot, pl.ds(part * half, half)]
                pltpu.make_async_copy(ref, target, sems.at[number]).start()


def await_block(buf, sems, slot, k):
    pltpu.make_async_copy(buf.at[slot], buf.at[slot], sems.at[k]).wait()


def latent_kernel(count, place_ref, *refs):
    row_refs, kv_refs, part_refs = refs[:count], refs[count : count + 4], refs[count + 4 : -4]
    rows_buf, kv_buf, row_sems, kv_sems = refs[-4:]
    place, plane = place_ref[0], place_ref[2]
    depth, piece = rows_buf.shape[1], kv_refs[0].shape[0]
    some = row_refs[0].shape[0]
    columns = pl.ds(pl.multiple_of(plane * depth, 128), depth)
    copies = [
        pltpu.make_async_copy(
            ref.at[:, columns], rows_buf.at[pl.ds(index * some, some)], row_sems.at[index]
        )
        for index, ref in enumerate(row_refs)
    ] + [
        pltpu.make_async_copy(ref, kv_buf.at[pl.ds((place ^ k) * piece, piece)], kv_sems.at[k])
        for k, ref in enumerate(kv_refs)
    ]
    for copy in copies:
        copy.start()
    for copy in copies:
        copy.wait()
    out = jnp.dot(rows_buf[...], kv_buf[...], preferred_element_type=jnp.float32)
    tok_rows = part_refs[0].shape[0]
    for index, ref in enumerate(part_refs):
        ref[...] = out[index * tok_rows : (index + 1) * tok_rows].astype(jnp.bfloat16)


def latent_parts(place, rows, kv_parts, tok_rows):
    height = sum(each.shape[0] for each in rows)
    piece, width = kv_parts[0].shape
    vmem, anywhere = pl.BlockSpec(memory_space=pltpu.VMEM), pl.BlockSpec(memory_space=pl.ANY)
    return pl.pallas_call(
        functools.partial(latent_kernel, len(rows)),
        out_shape=[pltpu.VMEM((tok_rows, width), jnp.bfloat16)] * (height // tok_rows),
        in_specs=[pl.BlockSpec(memory_space=pltpu.SMEM)]
        + [anywhere] * (len(rows) + len(kv_parts)),
        out_specs=[vmem] * (height // tok_rows),
        scratch_shapes=[
            pltpu.VMEM((height, GROUP * piece), jnp.bfloat16),
            pltpu.VMEM((GROUP * piece, width), jnp.bfloat16),
            pltpu.SemaphoreType.DMA((len(rows),)),
            pltpu.SemaphoreType.DMA((GROUP,)),
        ],
        compiler_params=pltpu.CompilerParams(vmem_limit_bytes=8 * MIB),
        cost_estimate=BRIEF,
        name="latent_parts",
    )(place, *rows, *kv_parts)


def hidden_kernel(place_ref, *refs):
    row_refs, gate_refs, up_refs, refs = refs[:4], refs[4:10], refs[10:16], refs[16:]
    down_refs, (hidden_ref, scale_ref, part_ref), refs = refs[:2], refs[2:5], refs[5:]
    rows_buf, gate_buf, up_buf, down_buf = refs[:4]
    row_sems, gate_sems, up_sems, down_sems = refs[4:]
    place, rep, plane = place_ref[0], place_ref[1], place_ref[2]
    core = place & 1
    tok_rows = row_refs[0].shape[0]
    row_copies, first = [], 0
    for index, ref in enumerate(row_refs):
        target = rows_buf.at[pl.ds(first, ref.shape[0])]
        row_copies.append(pltpu.make_async_copy(ref, target, row_sems.at[index]))
        first += ref.shape[0]

    def begin_slot(slot):
        begin_block(gate_refs, gate_buf, gate_sems, slot, place ^ slot, rep)
        begin_block(up_refs, up_buf, up_sems, slot, place ^ slot, rep)

    for copy in row_copies:
        copy.start()
    begin_slot(0)
    for copy in row_copies:
        copy.wait()
    begin_slot(1)

    features, units = gate_buf.shape[1:]
    terms = rows_buf[:, features:].astype(jnp.float32)
    lane = lax.broadcasted_iota(jnp.int32, terms.shape, 1)
    own = (lane >= 3 * plane) & (lane < 3 * plane + 3)
    scale_ref[...] = jnp.sum(jnp.where(own, terms, 0.0), axis=1, keepdims=True)

    for slot in range(GROUP):
        await_block(gate_buf, gate_sems, slot, place ^ slot)
        await_block(up_buf, up_sems, slot, place ^ slot)
        if slot + 2 < GROUP:
            begin_slot(slot + 2)
        else:
            begin_block(down_refs, down_buf, down_sems, slot - 2, core ^ (slot - 2), rep)
        rows = rows_buf[:, :features]
        gate_part = jnp.dot(rows, gate_buf[slot], preferred_element_type=jnp.float32)
        up_part = jnp.dot(rows, up_buf[slot], preferred_element_type=jnp.float32)
        hidden_ref[:, slot * units : (slot + 1) * units] = (
            gate_part / (1.0 + jnp.exp(-gate_part)) * up_part
        ).astype(jnp.bfloat16)

    for slot in range(2):
        await_block(down_buf, down_sems, slot, core ^ slot)
        width = down_buf.shape[2]
        part_ref[:, slot * width : (slot + 1) * width] = weighed(
            hidden_ref[2 * tok_rows : 3 * tok_rows],
            scale_ref[2 * tok_rows : 3 * tok_rows],
            down_buf[slot],
        )


def weighed(hidden, scale, down):
    out = jnp.dot(hidden, down, preferred_element_type=jnp.float32)
    return (out.astype(jnp.bfloat16).astype(jnp.float32) * scale).astype(jnp.bfloat16)


def hidden_units(place, rows, gates, ups, near):
    tok_rows, extended = rows[0].shape
    features, units = gates[0].shape
    columns = near[0].shape[1]
    hbm, vmem = pl.BlockSpec(memory_space=pltpu.HBM), pl.BlockSpec(memory_space=pltpu.VMEM)
    bf16, dma = jnp.bfloat16, pltpu.SemaphoreType.DMA
    operands = (*rows, *gates, *ups, *near)
    late = [rows[2], ups[3], ups[4], ups[5], gates[5]]
    specs = [
        pl.BlockSpec(memory_space=pl.ANY if any(each is one for one in late) else pltpu.HBM)
        for each in operands
    ]
    return pl.pallas_call(
        hidden_kernel,
        out_shape=[
            pltpu.VMEM((LINE * tok_rows, GROUP * units), bf16),
            pltpu.VMEM((LINE * tok_rows, 1), jnp.float32),
        ]
        + [pltpu.VMEM((tok_rows, 2 * columns), bf16)],
        in_specs=[pl.BlockSpec(memory_space=pltpu.SMEM)] + specs,
        out_specs=[vmem] * 3,
        scratch_shapes=[
            pltpu.VMEM((LINE * tok_rows, extended), bf16),
            pltpu.VMEM((GROUP, features, units), bf16),
            pltpu.VMEM((GROUP, features, units), bf16),
            pltpu.VMEM((2, GROUP * units, columns), bf16),
            dma((len(rows),)),
            dma((GROUP,)),
            dma((GROUP,)),
            dma((2,)),
        ],
        compiler_params=pltpu.CompilerParams(vmem_limit_bytes=52 * MIB),
        cost_estimate=BRIEF,
        name="hidden_units",
    )(place, *operands)


def rest_kernel(place_ref, hidden_ref, scale_ref, *refs):
    down_refs, (part0_ref, part1_ref, part3_ref, far_ref), (down_buf, sems) = refs[:6], refs[6:10], refs[10:]
    place, rep = place_ref[0], place_ref[1]

    def begin_slot(slot):
        begin_block(down_refs, down_buf, sems, slot, place ^ slot, rep)

    begin_slot(0)
    begin_slot(1)
    tok_rows, width = part0_ref.shape[0], down_buf.shape[2]
    for slot in range(GROUP):
        await_block(down_buf, sems, slot, place ^ slot)
        if slot + 2 < GROUP:
            begin_slot(slot + 2)
        out = weighed(hidden_ref[...], scale_ref[...], down_buf[slot])
        columns = slice(slot * width, (slot + 1) * width)
        for k, ref in ((0, part0_ref), (1, part1_ref), (3, part3_ref)):
            ref[:, columns] = out[k * tok_rows : (k + 1) * tok_rows]

        @pl.when((place ^ slot) >= 2)
        def _(slot=slot, out=out):
            columns = slice((slot % 2) * width, (slot % 2 + 1) * width)
            far_ref[:, columns] = out[2 * tok_rows : 3 * tok_rows]


def rest_products(place, hidden, scale, downs):
    tok_rows, units, width = hidden.shape[0] // LINE, hidden.shape[1], downs[0].shape[1]
    hbm, vmem = pl.BlockSpec(memory_space=pltpu.HBM), pl.BlockSpec(memory_space=pltpu.VMEM)
    return pl.pallas_call(
        rest_kernel,
        out_shape=[pltpu.VMEM((tok_rows, GROUP * width), jnp.bfloat16)] * 3
        + [pltpu.VMEM((tok_rows, 2 * width), jnp.bfloat16)],
        in_specs=[pl.BlockSpec(memory_space=pltpu.SMEM), vmem, vmem]
        + [hbm] * (len(downs) - 1)
        + [pl.BlockSpec(memory_space=pl.ANY)],
        out_specs=[vmem] * 4,
        scratch_shapes=[
            pltpu.VMEM((GROUP, units, width), jnp.bfloat16),
            pltpu.SemaphoreType.DMA((GROUP,)),
        ],
        compiler_params=pltpu.CompilerParams(vmem_limit_bytes=40 * MIB),
        cost_estimate=BRIEF,
        name="rest_products",
    )(place, hidden, scale, *downs)


def order_kernel(place_ref, blocks_ref, ordered_ref, sems):
    plane, chip, core = place_ref[0], place_ref[1], place_ref[2]
    count = sems.shape[0]
    rows = ordered_ref.shape[0] // count
    copies = []
    for source in range(count):
        far = ((source & 1) ^ core) * (count // 2) + ((source >> 1 & 1) ^ chip) * (count // 4)
        block = far + ((source >> 2) ^ plane)
        copies.append(
            pltpu.make_async_copy(
                blocks_ref.at[pl.ds(block * rows, rows)],
                ordered_ref.at[pl.ds(source * rows, rows)],
                sems.at[source],
            )
        )
    for copy in copies:
        copy.start()
    for copy in copies:
        copy.wait()


def in_source_order(place, blocks, rows):
    return pl.pallas_call(
        order_kernel,
        out_shape=jax.ShapeDtypeStruct(blocks.shape, blocks.dtype),
        in_specs=[
            pl.BlockSpec(memory_space=pltpu.SMEM),
            pl.BlockSpec(memory_space=pl.ANY),
        ],
        out_specs=pl.BlockSpec(memory_space=pltpu.VMEM),
        scratch_shapes=[pltpu.SemaphoreType.DMA((blocks.shape[0] // rows,))],
        compiler_params=pltpu.CompilerParams(vmem_limit_bytes=4 * MIB),
        cost_estimate=BRIEF,
        name="in_source_order",
    )(place, blocks)


def dense_shards(
    tokens,
    norm_gain,
    kv_weight,
    key_value_gain,
    gate_weight,
    up_weight,
    down_weight,
    expert_index,
    route_gate,
    owner,
):
    device_count = lax.axis_size("dev")
    push_cap = max(2, 2 * tokens.shape[0] // device_count)
    own_index = lax.axis_index("dev")
    plane, place = own_index // GROUP, own_index % GROUP
    place_info = jnp.stack([place, lax.axis_index("rep"), plane]).astype(jnp.int32)
    hold = lax.optimization_barrier

    def exchange(value, distance):
        return lax.ppermute(value, "dev", [(i, i ^ distance) for i in range(device_count)])

    def across_line(value, k):
        return exchange(value, GROUP * k)

    def other_core(value):
        return exchange(value, 1)

    def other_chip(value):
        return exchange(value, 2)

    def other_rep(value):
        return lax.ppermute(value, "rep", [(0, 1), (1, 0)])

    def narrow(value):
        return value.astype(jnp.bfloat16)

    def wide(value):
        return value.astype(jnp.float32)

    slots = cache_slots(owner, device_count, push_cap)

    kv_core, kv_x = other_core(kv_weight), other_chip(kv_weight)
    gate_core, up_core = other_core(gate_weight), other_core(up_weight)
    rows, gate_half = entry(
        place_info, tokens, norm_gain, expert_index, route_gate, gate_weight
    )
    rows, gate_core, up_core, kv_core, kv_x, up_own, down_own = hold(
        (rows, gate_core, up_core, kv_core, kv_x, up_weight, down_weight)
    )

    f = across_line(rows, 3)
    gate_x = other_chip(gate_half)
    down_core, kv_x_core = other_core(down_own), other_core(kv_x)
    up_half, down_half = halves_of(place_info, up_own, down_own)
    rows, up_half = hold((rows, up_half))
    a = across_line(rows, 1)
    gate_x, down_core, kv_x_core, up_half, down_half, slots = hold(
        (gate_x, down_core, kv_x_core, up_half, down_half, slots)
    )
    kv_parts = (kv_weight, kv_core, kv_x, kv_x_core)

    gate_y = other_rep(gate_x)
    up_x = other_chip(up_half)
    gate_x_core = other_core(gate_x)
    gate_y, up_x, gate_x_core, down_half = hold((gate_y, up_x, gate_x_core, down_half))

    c = across_line(f, 1)
    up_y = other_rep(up_x)
    down_x = other_chip(down_half)
    latent0, latent1, latent3 = latent_parts(
        place_info, (rows, a, f), kv_parts, tokens.shape[0]
    )
    gate_y_core, up_x_core = other_core(gate_y), other_core(up_x)
    c, up_y, down_x, gate_y_core, up_x_core, latent1, latent3 = hold(
        (c, up_y, down_x, gate_y_core, up_x_core, latent1, latent3)
    )

    up_y_core = other_core(up_y)
    down_y, down_x_core = other_rep(down_x), other_core(down_x)
    (latent2,) = latent_parts(place_info, (c,), kv_parts, tokens.shape[0])
    latents = [across_line(value, k) for k, value in ((1, latent1), (2, latent2), (3, latent3))]
    hidden, scale, near2 = hidden_units(
        place_info,
        (rows, a, c, f),
        (gate_weight, gate_core, gate_x, gate_y, gate_x_core, gate_y_core),
        (up_weight, up_core, up_x, up_y, up_x_core, up_y_core),
        (down_weight, down_core),
    )
    hidden, near2, latents, down_x_core = hold((hidden, near2, latents, down_x_core))
    near2_there = across_line(near2, 1)
    hidden, down_y = hold((hidden, down_y))
    down_y_core = other_core(down_y)
    part0, part1, part3, far2 = rest_products(
        place_info,
        hidden,
        scale,
        (down_weight, down_core, down_x, down_y, down_x_core, down_y_core),
    )
    far2_there = across_line(far2, 1)

    raw_latent = wide(latent0) + sum(wide(value) for value in latents)
    send_rows = cache_send_rows(
        latent_rows(raw_latent, key_value_gain), slots, device_count * push_cap
    )
    by_plane = send_rows.reshape(LINE, GROUP, push_cap, send_rows.shape[1])

    def for_plane(number):
        return lax.dynamic_index_in_dim(by_plane, number, 0, keepdims=False)

    there = [for_plane(plane)] + [across_line(for_plane(plane ^ k), k) for k in range(1, LINE)]

    part2_there = jnp.where(
        place & 2 == 2,
        jnp.concatenate([far2_there, near2_there], axis=1),
        jnp.concatenate([near2_there, far2_there], axis=1),
    )
    part_sum = narrow(wide(part3) + wide(part2_there))
    part_sum, part1, there = hold((part_sum, part1, there))
    there3, there1 = across_line(part_sum, 3), across_line(part1, 1)

    chip, core = place >> 1, place & 1
    by_chip = jnp.stack(there).reshape(LINE, 2, 2, push_cap, send_rows.shape[1])

    def for_chip(number):
        return lax.dynamic_index_in_dim(by_chip, number, 1, keepdims=False)

    by_core = jnp.stack([for_chip(chip), other_chip(for_chip(1 - chip))])

    def for_core(number):
        return lax.dynamic_index_in_dim(by_core, number, 2, keepdims=False)

    by_source = jnp.stack([for_core(core), other_core(for_core(1 - core))])
    latent_cache = in_source_order(
        jnp.stack([plane, chip, core]).astype(jnp.int32),
        by_source.reshape(device_count * push_cap, -1),
        push_cap,
    )
    moe_out = narrow(wide(part0) + wide(there1) + wide(there3))
    return (moe_out, latent_cache)


def solution(mesh):
    in_specs = (
        P(("rep", "dev"), None),
        P(),
        P("dev", None),
        P(),
        P(None, "dev"),
        P(None, "dev"),
        P("dev", None),
        P(("rep", "dev"), None),
        P(("rep", "dev"), None),
        P(("rep", "dev"), None),
    )
    out_specs = (P(("rep", "dev"), None), P(("rep", "dev"), None))
    dense = mesh.shape["dev"] == LINE * GROUP and mesh.shape["rep"] == 2
    shards = dense_shards if dense else packed_shards
    return jax.shard_map(shards, mesh=mesh, in_specs=in_specs, out_specs=out_specs, check_vma=False)
```
